512 devices in a mesh: row: 32 (over y, x), col: 16 (over z, core).
Axes of the slice: x: 4, y: 8, z: 8, core: 2. Of those that a mesh axis runs over, the one named last changes fastest.
Arguments:
- source: float32 [64, 32768], P(None, 'row'), may hold values from -8 to 8
- target: float32 [64, 32768], P(None, 'col'), may hold values from -8 to 8
Outputs:
- source_potential: float32 [32768], P('row')
- target_potential: float32 [32768], P('col')
- mapped: float32 [64, 32768], P(None, 'row')
The draws below stay inside these ranges and needn't reach their ends.
All inputs are finite; a program needn't handle non-finite values.
Results may differ from the reference program's by a relative error of at most 0.0003.
Values sent between devices are 32-bit elements; how exact they have to be, the bound alone decides.
A program may use at most 64 MiB of HBM per device.

```python
import jax
import jax.numpy as jnp
from jax import lax

D = 64
ITERS = 2
NS = 32768
NT = 32768


def target_field(key, strength):
    basic_field = jnp.clip(jax.random.normal(key, (D, NT), jnp.float32), -5.0, 5.0)
    position_class = jnp.arange(NT) % 8
    pair_weight = strength * (position_class == 1).astype(jnp.float32)
    drawn_weight = 1.0 - pair_weight
    blended = drawn_weight[None, :] * basic_field
    return jnp.clip(blended, -8.0, 8.0)


def draw_target(key, part):
    return target_field(key, 0.0)


def draw_source(key, part):
    strength = 0.0
    key = jax.random.fold_in(key, 3)
    private = jnp.clip(jax.random.normal(key, (D, NS), jnp.float32), -5.0, 5.0)
    index = jnp.arange(NS)
    position_class = index % 16
    exact_weight = strength * (position_class == 0).astype(jnp.float32)
    drawn_weight = 1.0 - exact_weight
    blended = drawn_weight[None, :] * private
    return jnp.clip(blended, -8.0, 8.0)


def setup_inputs(seed: int = 0) -> dict:
    splits = jax.random.split(jax.random.key(seed), 3)
    source = draw_source(jax.random.fold_in(splits[2], 71), 0)
    target = draw_target(jax.random.fold_in(splits[2], 71), 0)
    return {"source": source, "target": target}


EPSILON = 0.005

def normalize(points):
    return points / jnp.sqrt(lax.optimization_barrier(jnp.sum(points * points, axis=0, keepdims=True)) + 1e-06)

def cost_tile(left, right):
    left_sq = lax.optimization_barrier(jnp.sum(left * left, axis=0))
    right_sq = lax.optimization_barrier(jnp.sum(right * right, axis=0))
    inner = jnp.dot(left.T, right, precision=lax.Precision.HIGHEST, preferred_element_type=jnp.float32)
    return left_sq[:, None] + right_sq[None, :] - 2.0 * inner

def split_blocks(points):
    width = points.shape[1]
    block_len = min(256, width)
    count = width // block_len
    return points.reshape(points.shape[0], count, block_len).transpose(1, 0, 2)

def row_lse(left, right, potential):

    def one_block(block):
        scores = (potential[None, :] - cost_tile(block, right)) / EPSILON
        top = lax.optimization_barrier(jnp.max(scores, axis=1))
        return top + jnp.log(lax.optimization_barrier(jnp.sum(jnp.exp(scores - top[:, None]), axis=1)))
    return lax.map(one_block, split_blocks(left)).reshape(left.shape[1])

def reference(source, target):
    xs = normalize(source)
    ys = normalize(target)
    target_potential = jnp.zeros((ys.shape[1],), jnp.float32)
    source_potential = jnp.zeros((xs.shape[1],), jnp.float32)
    for step in range(ITERS):
        source_potential = -EPSILON * (row_lse(xs, ys, target_potential) - jnp.log(jnp.float32(NT)))
        target_potential = -EPSILON * (row_lse(ys, xs, source_potential) - jnp.log(jnp.float32(NS)))

    def map_block(block):
        scores = (target_potential[None, :] - cost_tile(block, ys)) / EPSILON
        top = lax.optimization_barrier(jnp.max(scores, axis=1))
        weight = jnp.exp(scores - top[:, None])
        numer = jnp.dot(ys, weight.T, precision=lax.Precision.HIGHEST, preferred_element_type=jnp.float32)
        return numer / lax.optimization_barrier(jnp.sum(weight, axis=1))[None, :]
    blocks = lax.map(map_block, split_blocks(xs))
    mapped = blocks.transpose(1, 0, 2).reshape(xs.shape[0], xs.shape[1])
    return (source_potential, target_potential, mapped)
```

```python
import functools
import math

import jax
import jax.numpy as jnp
from jax import lax
from jax.experimental import pallas as pl
from jax.experimental.pallas import tpu as pltpu
from jax.sharding import PartitionSpec as P

MESH = pl.DeviceIdType.MESH
ITERS = 2
EPSILON = 0.005
SCALE = 1.0 / (EPSILON * math.log(2.0))
UNSCALE = EPSILON * math.log(2.0)
LANES = 128
NZ, NX, NY = 8, 4, 8


def normalize(points):
    total = jnp.sum(points * points, axis=0, keepdims=True)
    return points / jnp.sqrt(total + 1e-06)


def split3(a):
    a1 = a.astype(jnp.bfloat16)
    r = a - a1.astype(jnp.float32)
    a2 = r.astype(jnp.bfloat16)
    a3 = (r - a2.astype(jnp.float32)).astype(jnp.bfloat16)
    return a1, a2, a3


def tree(op, xs):
    xs = list(xs)
    while len(xs) > 1:
        xs = [op(xs[i], xs[i + 1]) if i + 1 < len(xs) else xs[i] for i in range(0, len(xs), 2)]
    return xs[0]


def lse2(xs):
    top = tree(jnp.maximum, xs)
    return top + jnp.log2(tree(jnp.add, [jnp.exp2(x - top) for x in xs]))


def kernel(
    n_src_total,
    n_tgt_total,
    src,
    tgt,
    f_out,
    g_out,
    m_out,
    xk,
    yk,
    yt,
    score,
    nx,
    ny,
    gpot,
    fcol,
    part_m,
    part_p,
    a_loc,
    a_pair,
    a_sum,
    a_z,
    b_loc,
    b_x,
    b_sum,
    b_y,
    c_mine,
    c_give,
    c_pair,
    c_sum,
    c_z,
    c_res,
    c_all,
    c_half,
    s_ap,
    r_ap,
    s_az,
    r_az,
    s_bx,
    r_bx,
    s_by,
    r_by,
    s_cp,
    r_cp,
    s_cz,
    r_cz,
    s_cg,
    r_cg,
    s_ch,
    r_ch,
):
    d, ns = src.shape
    nt = tgt.shape[1]
    nsb, ntb = ns // LANES, nt // LANES
    row, col = lax.axis_index("row"), lax.axis_index("col")
    y, x = row // NX, row % NX
    z, core = col // 2, col % 2
    partner = (row, z * 2 + (1 - core))

    def z_peer(o):
        return (row, ((z + o) % NZ) * 2 + core)

    def x_peer(o):
        return (y * NX + (x + o) % NX, col)

    def y_peer(o):
        return (((y + o) % NY) * NX + x, col)

    peers = [partner]
    peers += [z_peer(o) for o in range(1, NZ)]
    peers += [x_peer(o) for o in range(1, NX)]
    peers += [y_peer(o) for o in range(1, NY)]
    barrier = pltpu.get_barrier_semaphore()
    for peer in peers:
        pl.semaphore_signal(barrier, inc=1, device_id=peer, device_id_type=MESH)

    def copy(src_ref, dst_ref, send, recv, peer):
        return pltpu.make_async_remote_copy(
            src_ref=src_ref, dst_ref=dst_ref, send_sem=send, recv_sem=recv,
            device_id=peer, device_id_type=MESH,
        )

    xs = normalize(src[...])
    nx_row = jnp.sum(xs * xs, axis=0, keepdims=True) * SCALE
    for b in range(nsb):
        nx[b : b + 1, :] = nx_row[:, b * LANES : (b + 1) * LANES]
    xs = xs * (2.0 * SCALE)
    first = lax.broadcasted_iota(jnp.int32, (LANES, LANES), 1) < d
    for b in range(nsb):
        blk = xs[:, b * LANES : (b + 1) * LANES]
        both = jnp.concatenate([blk, blk], axis=0).T
        x1 = both.astype(jnp.bfloat16).astype(jnp.float32)
        r = both - x1
        x2 = r.astype(jnp.bfloat16).astype(jnp.float32)
        rows = pl.ds(b * LANES, LANES)
        xk[rows, 0:128] = x1.astype(jnp.bfloat16)
        xk[rows, 128:256] = x2.astype(jnp.bfloat16)
        xk[rows, 256:384] = jnp.where(first, x1, r - x2).astype(jnp.bfloat16)
    ys = normalize(tgt[...])
    ny_row = jnp.sum(ys * ys, axis=0, keepdims=True) * SCALE
    for b in range(ntb):
        ny[b : b + 1, :] = ny_row[:, b * LANES : (b + 1) * LANES]
    y1, y2, y3 = split3(ys)
    for i, part in enumerate((y1, y2, y1, y2, y3, y1)):
        yk[i * d : (i + 1) * d, :] = part
    gpot[...] = -ny[...]
    lane = lax.broadcasted_iota(jnp.int32, (LANES, LANES), 1)
    for b in range(ntb):
        blk = ys[:, b * LANES : (b + 1) * LANES]
        both = jnp.concatenate([blk, blk], axis=0).T
        t1 = both.astype(jnp.bfloat16).astype(jnp.float32)
        r = both - t1
        t2 = r.astype(jnp.bfloat16).astype(jnp.float32)
        rows = pl.ds(b * LANES, LANES)
        yt[rows, 0:128] = jnp.where(first, t1, t2).astype(jnp.bfloat16)
        yt[rows, 128:256] = jnp.where(
            first, r - t2, jnp.where(lane == d, 1.0, 0.0)
        ).astype(jnp.bfloat16)

    def row_pass(with_scores):
        def block(b, _):
            base = pl.multiple_of(b * LANES, LANES)
            if with_scores:
                score[pl.ds(base, LANES), :] = jnp.dot(
                    xk[pl.ds(base, LANES), :], yk[...], preferred_element_type=jnp.float32
                )

            def group(q, _):
                rows = pl.ds(pl.multiple_of(base + q * 16, 16), 16)
                ts = [
                    score[rows, k * LANES : (k + 1) * LANES] + gpot[k : k + 1, :]
                    for k in range(ntb)
                ]
                top = tree(jnp.maximum, ts)
                part_m[rows, :] = top
                part_p[rows, :] = tree(jnp.add, [jnp.exp2(t - top) for t in ts])
                return 0

            lax.fori_loop(0, LANES // 16, group, 0, unroll=2)
            mt = part_m[pl.ds(base, LANES), :].T
            pt = part_p[pl.ds(base, LANES), :].T
            top = jnp.max(mt, axis=0, keepdims=True)
            tot = jnp.sum(pt * jnp.exp2(mt - top), axis=0, keepdims=True)
            a_loc[pl.ds(b, 1), :] = top + jnp.log2(tot)
            return 0

        lax.fori_loop(0, nsb, block, 0)

    def exchange_a(step):
        c = copy(a_loc, a_pair.at[step], s_ap.at[step], r_ap.at[step], partner)
        c.start()
        c.wait_recv()
        a_sum[step] = lse2([a_loc[...], a_pair[step]])
        cs = []
        for o in range(1, NZ):
            cz = copy(
                a_sum.at[step], a_z.at[step, z], s_az.at[step, o - 1], r_az.at[step, o - 1], z_peer(o)
            )
            cz.start()
            cs.append(cz)
        a_z[step, z] = a_sum[step]
        for cz in cs:
            cz.wait_recv()
        pot = math.log2(n_tgt_total) - lse2([a_z[step, i] for i in range(NZ)])
        c.wait_send()
        for cz in cs:
            cz.wait_send()
        return pot

    def col_pass():
        def chunk(k, _):
            lanes = pl.ds(pl.multiple_of(k * LANES, LANES), LANES)
            top = jnp.full((8, LANES), -jnp.inf, jnp.float32)
            acc = jnp.zeros((8, LANES), jnp.float32)
            for b in range(ns // LANES):
                ts = []
                for i in range(LANES // 8):
                    rows = slice(b * LANES + i * 8, b * LANES + (i + 1) * 8)
                    ts.append(score[rows, lanes] + fcol[rows, :])
                new = tree(jnp.maximum, ts)
                if b > 0:
                    new = jnp.maximum(new, top)
                add = tree(jnp.add, [jnp.exp2(t - new) for t in ts])
                acc = acc * jnp.exp2(top - new) + add if b > 0 else add
                top = new
            full = jnp.max(top, axis=0, keepdims=True)
            tot = jnp.sum(acc * jnp.exp2(top - full), axis=0, keepdims=True)
            b_loc[pl.ds(k, 1), :] = full + jnp.log2(tot)
            return 0

        lax.fori_loop(0, ntb, chunk, 0)

    def exchange_b(step):
        cs = []
        for o in range(1, NX):
            cx = copy(
                b_loc, b_x.at[step, x], s_bx.at[step, o - 1], r_bx.at[step, o - 1], x_peer(o)
            )
            cx.start()
            cs.append(cx)
        b_x[step, x] = b_loc[...]
        for cx in cs:
            cx.wait_recv()
        b_sum[step] = lse2([b_x[step, i] for i in range(NX)])
        for o in range(1, NY):
            cy = copy(
                b_sum.at[step], b_y.at[step, y], s_by.at[step, o - 1], r_by.at[step, o - 1], y_peer(o)
            )
            cy.start()
            cs.append(cy)
        b_y[step, y] = b_sum[step]
        for cy in cs[NX - 1 :]:
            cy.wait_recv()
        pot = math.log2(n_src_total) - lse2([b_y[step, i] for i in range(NY)])
        for cx in cs:
            cx.wait_send()
        return pot

    for step in range(ITERS):
        row_pass(step == 0)
        if step == 0:
            pl.semaphore_wait(barrier, len(peers))
        fpot = exchange_a(step)
        if step == ITERS - 1:
            f_out[...] = (fpot + nx[...]) * UNSCALE
        for b in range(nsb):
            fcol[b * LANES : (b + 1) * LANES, :] = jnp.broadcast_to(
                fpot[b : b + 1, :], (LANES, LANES)
            ).T
        col_pass()
        gpot[...] = exchange_b(step)
    g_out[...] = (gpot[...] + ny[...]) * UNSCALE

    half = d // 2

    def pair_copy(t, blk):
        return copy(c_give.at[blk], c_pair.at[blk], s_cp.at[t], r_cp.at[t], partner)

    def z_copy(o, blk):
        return copy(c_sum.at[blk], c_z.at[z], s_cz.at[o], r_cz.at[o], z_peer(o))

    def map_block(t, _):
        blk = (z + 1 + t) % NZ
        base = pl.multiple_of(blk * LANES, LANES)
        res = jnp.zeros((LANES, 2 * LANES), jnp.float32)
        w1s, w2s, tops = [], [], []
        for q in range(LANES // 16):
            rows = pl.ds(pl.multiple_of(base + q * 16, 16), 16)
            ts = [
                score[rows, k * LANES : (k + 1) * LANES] + gpot[k : k + 1, :] for k in range(ntb)
            ]
            top = jnp.max(tree(jnp.maximum, ts), axis=1, keepdims=True)
            w = jnp.concatenate([jnp.exp2(v - top) for v in ts], axis=1)
            w1 = w.astype(jnp.bfloat16)
            w1s.append(w1)
            w2s.append((w - w1.astype(jnp.float32)).astype(jnp.bfloat16))
            tops.append(jnp.broadcast_to(top, (16, LANES)))
        w1 = jnp.concatenate(w1s, axis=0)
        w2 = jnp.concatenate(w2s, axis=0)
        res = jnp.dot(w1, yt[...], preferred_element_type=jnp.float32)
        res += jnp.dot(w2, yt[...], preferred_element_type=jnp.float32)
        lo = res[:, :LANES].T
        hi = jnp.where(lane == d + 1, jnp.concatenate(tops, axis=0), res[:, LANES:]).T
        num = lo[:d] + lo[d:] + hi[:d]
        tail = hi[d : d + 8]
        mine = jnp.where(core == 0, num[:half], num[half:])
        give = jnp.where(core == 0, num[half:], num[:half])
        c_mine[blk, 0:half, :] = mine
        c_mine[blk, half : half + 8, :] = tail
        c_give[blk, 0:half, :] = give
        c_give[blk, half : half + 8, :] = tail
        pair_copy(t, blk).start()
        return 0

    def merge(parts):
        tops = [p[half + 1 : half + 2, :] for p in parts]
        top = tree(jnp.maximum, tops)
        tot = tree(jnp.add, [p[: half + 1, :] * jnp.exp2(v - top) for p, v in zip(parts, tops)])
        return tot, top

    def pair_merge(t, blk):
        pair_copy(t, blk).wait_recv()
        tot, top = merge([c_mine[blk], c_pair[blk]])
        c_sum[blk, 0 : half + 1, :] = tot
        c_sum[blk, half + 1 : half + 2, :] = top

    lax.fori_loop(0, NZ, map_block, 0)

    def send_block(t, _):
        blk = (z + 1 + t) % NZ
        pair_merge(t, blk)
        z_copy(t + 1, blk).start()
        return 0

    lax.fori_loop(0, NZ - 1, send_block, 0)
    pair_merge(NZ - 1, z)
    c_z[z] = c_sum[z]
    for o in range(1, NZ):
        z_copy(o, (z + o) % NZ).wait_recv()
    tot, _ = merge([c_z[i] for i in range(NZ)])
    c_res[...] = tot[:half] / tot[half : half + 1]

    def gather_copy(o):
        return copy(c_res, c_all.at[z], s_cg.at[o], r_cg.at[o], z_peer(o))

    for o in range(1, NZ):
        gather_copy(o).start()
    c_all[z] = c_res[...]
    for o in range(1, NZ):
        gather_copy(o).wait_recv()
    last = copy(c_all, c_half, s_ch.at[0], r_ch.at[0], partner)
    last.start()
    for t in range(NZ):
        pair_copy(t, (z + 1 + t) % NZ).wait_send()
    for o in range(1, NZ):
        z_copy(o, (z + o) % NZ).wait_send()
        gather_copy(o).wait_send()
    last.wait_recv()
    for b in range(NZ):
        own, other = c_all[b], c_half[b]
        lanes = slice(b * LANES, (b + 1) * LANES)
        m_out[0:half, lanes] = jnp.where(core == 0, own, other)
        m_out[half:d, lanes] = jnp.where(core == 0, other, own)
    last.wait_send()


def solution(mesh):
    nrow, ncol = mesh.shape["row"], mesh.shape["col"]

    def shards(source, target):
        d, ns = source.shape
        nt = target.shape[1]
        nsb, ntb = ns // LANES, nt // LANES
        half = d // 2
        f32, bf16 = jnp.float32, jnp.bfloat16
        vmem = pltpu.VMEM
        dma = pltpu.SemaphoreType.DMA
        f, g, m = pl.pallas_call(
            functools.partial(kernel, ns * nrow, nt * ncol),
            out_shape=(
                jax.ShapeDtypeStruct((nsb, LANES), f32),
                jax.ShapeDtypeStruct((ntb, LANES), f32),
                jax.ShapeDtypeStruct((d, ns), f32),
            ),
            in_specs=[pl.BlockSpec(memory_space=vmem)] * 2,
            out_specs=(pl.BlockSpec(memory_space=vmem),) * 3,
            scratch_shapes=[
                vmem((ns, 6 * d), bf16),
                vmem((6 * d, nt), bf16),
                vmem((nt, 2 * LANES), bf16),
                vmem((ns, nt), f32),
                vmem((nsb, LANES), f32),
                vmem((ntb, LANES), f32),
                vmem((ntb, LANES), f32),
                vmem((ns, LANES), f32),
                vmem((ns, LANES), f32),
                vmem((ns, LANES), f32),
                vmem((nsb, LANES), f32),
                vmem((ITERS, nsb, LANES), f32),
                vmem((ITERS, nsb, LANES), f32),
                vmem((ITERS, NZ, nsb, LANES), f32),
                vmem((ntb, LANES), f32),
                vmem((ITERS, NX, ntb, LANES), f32),
                vmem((ITERS, ntb, LANES), f32),
                vmem((ITERS, NY, ntb, LANES), f32),
                vmem((NZ, half + 8, LANES), f32),
                vmem((NZ, half + 8, LANES), f32),
                vmem((NZ, half + 8, LANES), f32),
                vmem((NZ, half + 8, LANES), f32),
                vmem((NZ, half + 8, LANES), f32),
                vmem((half, LANES), f32),
                vmem((NZ, half, LANES), f32),
                vmem((NZ, half, LANES), f32),
                dma((ITERS,)),
                dma((ITERS,)),
                dma((ITERS, NZ - 1)),
                dma((ITERS, NZ - 1)),
                dma((ITERS, NX - 1)),
                dma((ITERS, NX - 1)),
                dma((ITERS, NY - 1)),
                dma((ITERS, NY - 1)),
                dma((NZ,)),
                dma((NZ,)),
                dma((NZ,)),
                dma((NZ,)),
                dma((NZ,)),
                dma((NZ,)),
                dma((1,)),
                dma((1,)),
            ],
            compiler_params=pltpu.CompilerParams(
                collective_id=0, has_side_effects=True, vmem_limit_bytes=40 * 2**20
            ),
            name="sinkhorn",
        )(source, target)
        return f.reshape(ns), g.reshape(nt), m

    return jax.shard_map(
        shards,
        mesh=mesh,
        in_specs=(P(None, "row"), P(None, "col")),
        out_specs=(P("row"), P("col"), P(None, "row")),
        check_vma=False,
    )
```

```python
import functools
import math

import jax
import jax.numpy as jnp
from jax import lax
from jax.experimental import pallas as pl
from jax.experimental.pallas import tpu as pltpu
from jax.sharding import PartitionSpec as P

MESH = pl.DeviceIdType.MESH
ITERS = 2
EPSILON = 0.005
SCALE = 1.0 / (EPSILON * math.log(2.0))
UNSCALE = EPSILON * math.log(2.0)
LANES = 128
NZ, NX, NY = 8, 4, 8
NC, NR = 2 * NZ, NX * NY
ROW_CHUNKS, COL_CHUNKS = 2, 4


def normalize(points):
    total = jnp.sum(points * points, axis=0, keepdims=True)
    return points / jnp.sqrt(total + 1e-06)


def split3(a):
    a1 = a.astype(jnp.bfloat16)
    r = a - a1.astype(jnp.float32)
    a2 = r.astype(jnp.bfloat16)
    a3 = (r - a2.astype(jnp.float32)).astype(jnp.bfloat16)
    return a1, a2, a3


def tree(op, xs):
    xs = list(xs)
    while len(xs) > 1:
        xs = [op(xs[i], xs[i + 1]) if i + 1 < len(xs) else xs[i] for i in range(0, len(xs), 2)]
    return xs[0]


def lse2(xs):
    top = tree(jnp.maximum, xs)
    return top + jnp.log2(tree(jnp.add, [jnp.exp2(x - top) for x in xs]))


def hops(o, n):
    return min(o, n - o)


def kernel(
    n_src_total,
    n_tgt_total,
    src_hbm,
    tgt_hbm,
    f_out,
    g_out,
    m_out,
    src,
    tgt,
    xk,
    yk,
    yt,
    score,
    nx,
    ny,
    gpot,
    fcol,
    part_m,
    part_p,
    a_loc,
    a_all,
    b_loc,
    b_all,
    wbuf,
    c_msg,
    c_in,
    c_res,
    c_all,
    load,
    s_a,
    r_a,
    s_b,
    r_b,
    s_c,
    r_c,
    s_g,
    r_g,
):
    d, ns = src.shape
    nt = tgt.shape[1]
    nsb, ntb = ns // LANES, nt // LANES
    row, col = lax.axis_index("row"), lax.axis_index("col")
    y, x = row // NX, row % NX
    z, core = col // 2, col % 2

    load_src = pltpu.make_async_copy(src_hbm, src, load.at[0])
    load_tgt = pltpu.make_async_copy(tgt_hbm, tgt, load.at[1])
    load_src.start()
    load_tgt.start()

    col_peers = [(o, k) for o in range(NZ) for k in range(2) if (o, k) != (0, 0)]
    col_peers.sort(key=lambda p: -hops(p[0], NZ))
    row_peers = [(o, k) for o in range(NY) for k in range(NX) if (o, k) != (0, 0)]
    row_peers.sort(key=lambda p: -hops(p[0], NY) - hops(p[1], NX))

    def col_peer(o, k):
        return (row, ((z + o) % NZ) * 2 + (core + k) % 2)

    def row_peer(o, k):
        return (((y + o) % NY) * NX + (x + k) % NX, col)

    peers = [col_peer(*p) for p in col_peers] + [row_peer(*p) for p in row_peers]
    barrier = pltpu.get_barrier_semaphore()
    for peer in peers:
        pl.semaphore_signal(barrier, inc=1, device_id=peer, device_id_type=MESH)

    def copy(src_ref, dst_ref, send, recv, peer):
        return pltpu.make_async_remote_copy(
            src_ref=src_ref, dst_ref=dst_ref, send_sem=send, recv_sem=recv,
            device_id=peer, device_id_type=MESH,
        )

    load_src.wait()
    xs = normalize(src[...])
    nx_row = jnp.sum(xs * xs, axis=0, keepdims=True) * SCALE
    for b in range(nsb):
        nx[b : b + 1, :] = nx_row[:, b * LANES : (b + 1) * LANES]
    xs = xs * (2.0 * SCALE)
    first = lax.broadcasted_iota(jnp.int32, (LANES, LANES), 1) < d
    lane = lax.broadcasted_iota(jnp.int32, (LANES, LANES), 1)
    for b in range(nsb):
        blk = xs[:, b * LANES : (b + 1) * LANES]
        both = jnp.concatenate([blk, blk], axis=0).T
        x1 = both.astype(jnp.bfloat16).astype(jnp.float32)
        r = both - x1
        x2 = r.astype(jnp.bfloat16).astype(jnp.float32)
        rows = pl.ds(b * LANES, LANES)
        xk[rows, 0:128] = x1.astype(jnp.bfloat16)
        xk[rows, 128:256] = x2.astype(jnp.bfloat16)
        xk[rows, 256:384] = jnp.where(first, x1, r - x2).astype(jnp.bfloat16)
    load_tgt.wait()
    ys = normalize(tgt[...])
    tgt[...] = ys
    ny_row = jnp.sum(ys * ys, axis=0, keepdims=True) * SCALE
    for b in range(ntb):
        ny[b : b + 1, :] = ny_row[:, b * LANES : (b + 1) * LANES]
    y1, y2, y3 = split3(ys)
    for i, part in enumerate((y1, y2, y1, y2, y3, y1)):
        yk[i * d : (i + 1) * d, :] = part
    gpot[...] = -ny[...]

    def build_map_operand():
        for b in range(ntb):
            blk = tgt[:, b * LANES : (b + 1) * LANES]
            both = jnp.concatenate([blk, blk], axis=0).T
            t1 = both.astype(jnp.bfloat16).astype(jnp.float32)
            r = both - t1
            t2 = r.astype(jnp.bfloat16).astype(jnp.float32)
            rows = pl.ds(b * LANES, LANES)
            yt[rows, 0:128] = jnp.where(first, t1, t2).astype(jnp.bfloat16)
            yt[rows, 128:256] = jnp.where(
                first, r - t2, jnp.where(lane == d, 1.0, 0.0)
            ).astype(jnp.bfloat16)

    def row_pass(step):
        blocks = nsb // ROW_CHUNKS
        size = blocks * LANES
        for c in range(ROW_CHUNKS):
            if step == 0:
                rows = slice(c * size, (c + 1) * size)
                score[rows, :] = jnp.dot(
                    xk[rows, :], yk[...], preferred_element_type=jnp.float32
                )

            def group(q, _):
                rows = pl.ds(pl.multiple_of(c * size + q * 16, 16), 16)
                ts = [
                    score[rows, k * LANES : (k + 1) * LANES] + gpot[k : k + 1, :]
                    for k in range(ntb)
                ]
                top = tree(jnp.maximum, ts)
                part_m[rows, :] = top
                part_p[rows, :] = tree(jnp.add, [jnp.exp2(t - top) for t in ts])
                return 0

            lax.fori_loop(0, size // 16, group, 0, unroll=8)
            for b in range(c * blocks, (c + 1) * blocks):
                mt = part_m[b * LANES : (b + 1) * LANES, :].T
                pt = part_p[b * LANES : (b + 1) * LANES, :].T
                top = jnp.max(mt, axis=0, keepdims=True)
                tot = jnp.sum(pt * jnp.exp2(mt - top), axis=0, keepdims=True)
                a_loc[step, b : b + 1, :] = top + jnp.log2(tot)
            if step == 0 and c == 0:
                pl.semaphore_wait(barrier, len(peers))
            part = pl.ds(c * blocks, blocks)
            for o, k in col_peers:
                copy(
                    a_loc.at[step, part], a_all.at[step, col, part],
                    s_a.at[step], r_a.at[step], col_peer(o, k),
                ).start()

    def finish_a(step):
        a_all[step, col] = a_loc[step]
        got = a_all.at[step, 0 : NC - 1]
        whole = copy(got, got, s_a.at[step], r_a.at[step], peers[0])
        whole.wait_recv()
        pot = math.log2(n_tgt_total) - lse2([a_all[step, i] for i in range(NC)])
        for b in range(nsb):
            fcol[b * LANES : (b + 1) * LANES, :] = jnp.broadcast_to(
                pot[b : b + 1, :], (LANES, LANES)
            ).T
        if step == ITERS - 1:
            f_out[...] = (pot + nx[...]) * UNSCALE

    def col_pass(step):
        blocks = ntb // COL_CHUNKS
        for c in range(COL_CHUNKS):

            def chunk(k, _):
                lanes = pl.ds(pl.multiple_of(k * LANES, LANES), LANES)
                top = acc = None
                for b in range(ns // 64):
                    ts = []
                    for i in range(8):
                        rows = slice(b * 64 + i * 8, b * 64 + (i + 1) * 8)
                        ts.append(score[rows, lanes] + fcol[rows, :])
                    new = tree(jnp.maximum, ts)
                    if b > 0:
                        new = jnp.maximum(new, top)
                    add = tree(jnp.add, [jnp.exp2(t - new) for t in ts])
                    acc = acc * jnp.exp2(top - new) + add if b > 0 else add
                    top = new
                full = jnp.max(top, axis=0, keepdims=True)
                tot = jnp.sum(acc * jnp.exp2(top - full), axis=0, keepdims=True)
                b_loc[step, pl.ds(k, 1), :] = full + jnp.log2(tot)
                return 0

            lax.fori_loop(c * blocks, (c + 1) * blocks, chunk, 0, unroll=2)
            part = pl.ds(c * blocks, blocks)
            for o, k in row_peers:
                copy(
                    b_loc.at[step, part], b_all.at[step, row, part],
                    s_b.at[step], r_b.at[step], row_peer(o, k),
                ).start()

    def finish_b(step):
        b_all[step, row] = b_loc[step]
        got = b_all.at[step, 0 : NR - 1]
        copy(got, got, s_b.at[step], r_b.at[step], peers[0]).wait_recv()
        pot = math.log2(n_src_total) - lse2([b_all[step, i] for i in range(NR)])
        gpot[...] = pot
        if step == ITERS - 1:
            g_out[...] = (pot + ny[...]) * UNSCALE

    for step in range(ITERS):
        row_pass(step)
        if step == 0:
            build_map_operand()
        finish_a(step)
        col_pass(step)
        finish_b(step)

    half = d // 2
    tail = half + 8
    tops_of = [None] * NZ

    def weights(t):
        base = pl.multiple_of((z + 1 + t) % NZ * LANES, LANES)
        tops = []
        for q in range(LANES // 16):
            rows = pl.ds(pl.multiple_of(base + q * 16, 16), 16)
            ts = [
                score[rows, k * LANES : (k + 1) * LANES] + gpot[k : k + 1, :] for k in range(ntb)
            ]
            top = jnp.max(tree(jnp.maximum, ts), axis=1, keepdims=True)
            for k, v in enumerate(ts):
                w = jnp.exp2(v - top)
                w1 = w.astype(jnp.bfloat16)
                lanes = slice(k * LANES, (k + 1) * LANES)
                wbuf[t % 2, q * 16 : (q + 1) * 16, lanes] = w1
                wbuf[t % 2, LANES + q * 16 : LANES + (q + 1) * 16, lanes] = (
                    w - w1.astype(jnp.float32)
                ).astype(jnp.bfloat16)
            tops.append(jnp.broadcast_to(top, (16, LANES)))
        tops_of[t] = jnp.concatenate(tops, axis=0)

    def send_block(t):
        blk = (z + 1 + t) % NZ
        both = jnp.dot(wbuf[t % 2], yt[...], preferred_element_type=jnp.float32)
        res = both[:LANES] + both[LANES:]
        lo = res[:, :LANES].T
        hi = jnp.where(lane == d + 1, tops_of[t], res[:, LANES:]).T
        num = lo[:d] + lo[d:] + hi[:d]
        for k in range(2):
            c_msg[t, k, 0:half, :] = num[k * half : (k + 1) * half]
            c_msg[t, k, half:tail, :] = hi[d : d + 8]
        for k in range(2):
            if (t, k) != (NZ - 1, 0):
                copy(
                    c_msg.at[t, (core + k) % 2], c_in.at[col], s_c.at[0], r_c.at[0],
                    col_peer(t + 1, k),
                ).start()

    weights(0)
    for t in range(NZ):
        if t + 1 < NZ:
            weights(t + 1)
        send_block(t)
    c_in[col] = c_msg[NZ - 1, core]
    got = c_in.at[0 : NC - 1]
    c_whole = copy(got, got, s_c.at[0], r_c.at[0], peers[0])
    c_whole.wait_recv()
    tops = [c_in[i, half + 1 : half + 2, :] for i in range(NC)]
    top = tree(jnp.maximum, tops)
    tot = tree(
        jnp.add, [c_in[i, 0 : half + 1, :] * jnp.exp2(tops[i] - top) for i in range(NC)]
    )
    c_res[...] = tot[:half] / tot[half : half + 1]
    for o, k in col_peers:
        copy(c_res, c_all.at[col], s_g.at[0], r_g.at[0], col_peer(o, k)).start()
    c_all[col] = c_res[...]
    got = c_all.at[0 : NC - 1]
    g_whole = copy(got, got, s_g.at[0], r_g.at[0], peers[0])

    for step in range(ITERS):
        a_got, b_got = a_all.at[step, 0 : NC - 1], b_all.at[step, 0 : NR - 1]
        copy(a_got, a_got, s_a.at[step], r_a.at[step], peers[0]).wait_send()
        copy(b_got, b_got, s_b.at[step], r_b.at[step], peers[0]).wait_send()
    c_whole.wait_send()
    g_whole.wait_recv()
    for i in range(NC):
        m_out[i % 2 * half : (i % 2 + 1) * half, i // 2 * LANES : (i // 2 + 1) * LANES] = c_all[i]
    g_whole.wait_send()


def solution(mesh):
    nrow, ncol = mesh.shape["row"], mesh.shape["col"]

    def shards(source, target):
        d, ns = source.shape
        nt = target.shape[1]
        nsb, ntb = ns // LANES, nt // LANES
        half = d // 2
        f32, bf16 = jnp.float32, jnp.bfloat16
        vmem = pltpu.VMEM
        dma = pltpu.SemaphoreType.DMA
        f, g, m = pl.pallas_call(
            functools.partial(kernel, ns * nrow, nt * ncol),
            out_shape=(
                jax.ShapeDtypeStruct((nsb, LANES), f32),
                jax.ShapeDtypeStruct((ntb, LANES), f32),
                jax.ShapeDtypeStruct((d, ns), f32),
            ),
            in_specs=[pl.BlockSpec(memory_space=pl.ANY)] * 2,
            out_specs=(pl.BlockSpec(memory_space=vmem),) * 3,
            scratch_shapes=[
                vmem((d, ns), f32),
                vmem((d, nt), f32),
                vmem((ns, 6 * d), bf16),
                vmem((6 * d, nt), bf16),
                vmem((nt, 2 * LANES), bf16),
                vmem((ns, nt), f32),
                vmem((nsb, LANES), f32),
                vmem((ntb, LANES), f32),
                vmem((ntb, LANES), f32),
                vmem((ns, LANES), f32),
                vmem((ns, LANES), f32),
                vmem((ns, LANES), f32),
                vmem((ITERS, nsb, LANES), f32),
                vmem((ITERS, NC, nsb, LANES), f32),
                vmem((ITERS, ntb, LANES), f32),
                vmem((ITERS, NR, ntb, LANES), f32),
                vmem((2, 2 * LANES, nt), bf16),
                vmem((NZ, 2, half + 8, LANES), f32),
                vmem((NC, half + 8, LANES), f32),
                vmem((half, LANES), f32),
                vmem((NC, half, LANES), f32),
                dma((2,)),
                dma((ITERS,)),
                dma((ITERS,)),
                dma((ITERS,)),
                dma((ITERS,)),
                dma((1,)),
                dma((1,)),
                dma((1,)),
                dma((1,)),
            ],
            compiler_params=pltpu.CompilerParams(
                collective_id=0, has_side_effects=True, vmem_limit_bytes=40 * 2**20
            ),
            name="sinkhorn",
        )(source, target)
        return f.reshape(ns), g.reshape(nt), m

    return jax.shard_map(
        shards,
        mesh=mesh,
        in_specs=(P(None, "row"), P(None, "col")),
        out_specs=(P("row"), P("col"), P(None, "row")),
        check_vma=False,
    )
```

```python
import functools
import math

import jax
import jax.numpy as jnp
from jax import lax
from jax.experimental import pallas as pl
from jax.experimental.pallas import tpu as pltpu
from jax.sharding import PartitionSpec as P

MESH = pl.DeviceIdType.MESH
ITERS = 2
EPSILON = 0.005
SCALE = 1.0 / (EPSILON * math.log(2.0))
UNSCALE = EPSILON * math.log(2.0)
LANES = 128
NZ, NX, NY = 8, 4, 8
NC, NR = 2 * NZ, NX * NY
PARTS = 2


def normalize(points):
    total = jnp.sum(points * points, axis=0, keepdims=True)
    return points / jnp.sqrt(total + 1e-06)


def split3(a):
    a1 = a.astype(jnp.bfloat16)
    r = a - a1.astype(jnp.float32)
    a2 = r.astype(jnp.bfloat16)
    a3 = (r - a2.astype(jnp.float32)).astype(jnp.bfloat16)
    return a1, a2, a3


def tree(op, xs):
    xs = list(xs)
    while len(xs) > 1:
        xs = [op(xs[i], xs[i + 1]) if i + 1 < len(xs) else xs[i] for i in range(0, len(xs), 2)]
    return xs[0]


def lse2(xs):
    top = tree(jnp.maximum, xs)
    return top + jnp.log2(tree(jnp.add, [jnp.exp2(x - top) for x in xs]))


def hops(o, n):
    return min(o, n - o)


def kernel(
    n_src_total,
    n_tgt_total,
    src_hbm,
    tgt_hbm,
    f_out,
    g_out,
    m_out,
    src,
    tgt,
    xk,
    yk,
    yt,
    score,
    nx,
    ny,
    gpot,
    fcol,
    part_m,
    part_p,
    col_m,
    col_p,
    a_loc,
    a_all,
    b_loc,
    b_all,
    wbuf,
    c_mine,
    c_give,
    c_pair,
    c_sum,
    c_in,
    c_res,
    c_all,
    load,
    s_a,
    r_a,
    s_b,
    r_b,
    s_p,
    r_p,
    s_c,
    r_c,
    s_g,
    r_g,
):
    d, ns = src.shape
    nt = tgt.shape[1]
    nsb, ntb = ns // LANES, nt // LANES
    row, col = lax.axis_index("row"), lax.axis_index("col")
    y, x = row // NX, row % NX
    z, core = col // 2, col % 2

    load_src = pltpu.make_async_copy(src_hbm, src, load.at[0])
    load_tgt = pltpu.make_async_copy(tgt_hbm, tgt, load.at[1])
    load_src.start()
    load_tgt.start()

    col_peers = [(o, k) for o in range(NZ) for k in range(2) if (o, k) != (0, 0)]
    col_peers.sort(key=lambda p: -hops(p[0], NZ))
    row_peers = [(o, k) for o in range(NY) for k in range(NX) if (o, k) != (0, 0)]
    row_peers.sort(key=lambda p: -hops(p[0], NY) - hops(p[1], NX))

    def col_peer(o, k):
        return (row, ((z + o) % NZ) * 2 + (core + k) % 2)

    def row_peer(o, k):
        return (((y + o) % NY) * NX + (x + k) % NX, col)

    peers = [col_peer(*p) for p in col_peers] + [row_peer(*p) for p in row_peers]
    barrier = pltpu.get_barrier_semaphore()
    for peer in peers:
        pl.semaphore_signal(barrier, inc=1, device_id=peer, device_id_type=MESH)

    def copy(src_ref, dst_ref, send, recv, peer):
        return pltpu.make_async_remote_copy(
            src_ref=src_ref, dst_ref=dst_ref, send_sem=send, recv_sem=recv,
            device_id=peer, device_id_type=MESH,
        )

    load_src.wait()
    xs = normalize(src[...])
    nx_row = jnp.sum(xs * xs, axis=0, keepdims=True) * SCALE
    for b in range(nsb):
        nx[b : b + 1, :] = nx_row[:, b * LANES : (b + 1) * LANES]
    xs = xs * (2.0 * SCALE)
    first = lax.broadcasted_iota(jnp.int32, (LANES, LANES), 1) < d
    lane = lax.broadcasted_iota(jnp.int32, (LANES, LANES), 1)
    for b in range(nsb):
        blk = xs[:, b * LANES : (b + 1) * LANES]
        both = jnp.concatenate([blk, blk], axis=0).T
        x1 = both.astype(jnp.bfloat16).astype(jnp.float32)
        r = both - x1
        x2 = r.astype(jnp.bfloat16).astype(jnp.float32)
        rows = pl.ds(b * LANES, LANES)
        xk[rows, 0:128] = x1.astype(jnp.bfloat16)
        xk[rows, 128:256] = x2.astype(jnp.bfloat16)
        xk[rows, 256:384] = jnp.where(first, x1, r - x2).astype(jnp.bfloat16)
    load_tgt.wait()
    ys = normalize(tgt[...])
    tgt[...] = ys
    ny_row = jnp.sum(ys * ys, axis=0, keepdims=True) * SCALE
    for b in range(ntb):
        ny[b : b + 1, :] = ny_row[:, b * LANES : (b + 1) * LANES]
    y1, y2, y3 = split3(ys)
    for i, part in enumerate((y1, y2, y1, y2, y3, y1)):
        yk[i * d : (i + 1) * d, :] = part
    gpot[...] = -ny[...]

    def build_map_operand():
        for b in range(ntb):
            blk = tgt[:, b * LANES : (b + 1) * LANES]
            both = jnp.concatenate([blk, blk], axis=0).T
            t1 = both.astype(jnp.bfloat16).astype(jnp.float32)
            r = both - t1
            t2 = r.astype(jnp.bfloat16).astype(jnp.float32)
            rows = pl.ds(b * LANES, LANES)
            yt[rows, 0:128] = jnp.where(first, t1, t2).astype(jnp.bfloat16)
            yt[rows, 128:256] = jnp.where(
                first, r - t2, jnp.where(lane == d, 1.0, 0.0)
            ).astype(jnp.bfloat16)

    def score_tiles(c):
        rows = slice(c * 256, (c + 1) * 256)
        for n in range(nt // 256):
            lanes = slice(n * 256, (n + 1) * 256)

            def tile():
                score[rows, lanes] = jnp.dot(
                    xk[rows, :], yk[:, lanes], preferred_element_type=jnp.float32
                )

            yield tile

    def row_group(base, size, lo, hi, carry):
        rows = pl.ds(base, size)
        ts = [score[rows, k * LANES : (k + 1) * LANES] + gpot[k : k + 1, :] for k in range(lo, hi)]
        top = tree(jnp.maximum, ts)
        if carry:
            old = part_m[rows, :]
            top = jnp.maximum(top, old)
        tot = tree(jnp.add, [jnp.exp2(t - top) for t in ts])
        if carry:
            tot += part_p[rows, :] * jnp.exp2(old - top)
        part_m[rows, :] = top
        part_p[rows, :] = tot

    def send_rows(step, c):
        for i in range(nsb // PARTS):
            b = c * (nsb // PARTS) + i
            mt = part_m[b * LANES : (b + 1) * LANES, :].T
            pt = part_p[b * LANES : (b + 1) * LANES, :].T
            top = jnp.max(mt, axis=0, keepdims=True)
            tot = jnp.sum(pt * jnp.exp2(mt - top), axis=0, keepdims=True)
            a_loc[step, c, i : i + 1, :] = top + jnp.log2(tot)
        if step == 0 and c == 0:
            pl.semaphore_wait(barrier, len(peers))
        for o, k in col_peers:
            copy(
                a_loc.at[step, c], a_all.at[step, c, col],
                s_a.at[step], r_a.at[step, c], col_peer(o, k),
            ).start()

    def first_row_pass():
        count = ns // 256
        for c in range(count + 1):
            tiles = score_tiles(c) if c < count else [lambda: None] * (nt // 256)
            for n, tile in enumerate(tiles):
                tile()
                if c > 0:
                    for q in range(2):
                        row_group((c - 1) * 256 + n * 32 + q * 16, 16, 0, ntb, False)
            if c > 0 and c % (count // PARTS) == 0:
                send_rows(0, c // (count // PARTS) - 1)

    def later_row_pass(step):
        wide = ntb // PARTS
        for c in range(PARTS):
            receive_b(step - 1, c)
            size = ns // PARTS
            for h in range(PARTS):

                def group(q, _):
                    base = pl.multiple_of(h * size + q * 32, 32)
                    row_group(base, 32, c * wide, (c + 1) * wide, c > 0)
                    return 0

                lax.fori_loop(0, size // 32, group, 0, unroll=8)
                if c == PARTS - 1:
                    send_rows(step, h)

    def receive_a(step, c):
        a_all[step, c, col] = a_loc[step, c]
        got = a_all.at[step, c, 0 : NC - 1]
        copy(got, got, s_a.at[step], r_a.at[step, c], peers[0]).wait_recv()
        pot = math.log2(n_tgt_total) - lse2([a_all[step, c, i] for i in range(NC)])
        size = nsb // PARTS
        for i in range(size):
            b = c * size + i
            fcol[b * LANES : (b + 1) * LANES, :] = jnp.broadcast_to(
                pot[i : i + 1, :], (LANES, LANES)
            ).T
        if step == ITERS - 1:
            part = slice(c * size, (c + 1) * size)
            f_out[part, :] = (pot + nx[part, :]) * UNSCALE

    def col_pass(step):
        wide = ntb // PARTS
        size = ns // PARTS
        for h in range(PARTS):
            receive_a(step, h)
            for c in range(PARTS):
                tops, accs = [None] * wide, [None] * wide
                if h > 0:
                    for k in range(wide):
                        lanes = slice((c * wide + k) * LANES, (c * wide + k + 1) * LANES)
                        tops[k], accs[k] = col_m[:, lanes], col_p[:, lanes]
                for b in range(size // 64):
                    for k in range(wide):
                        lanes = slice((c * wide + k) * LANES, (c * wide + k + 1) * LANES)
                        ts = []
                        for i in range(8):
                            at = h * size + b * 64 + i * 8
                            ts.append(score[at : at + 8, lanes] + fcol[at : at + 8, :])
                        new = tree(jnp.maximum, ts)
                        if tops[k] is not None:
                            new = jnp.maximum(new, tops[k])
                        add = tree(jnp.add, [jnp.exp2(t - new) for t in ts])
                        if tops[k] is not None:
                            add += accs[k] * jnp.exp2(tops[k] - new)
                        tops[k], accs[k] = new, add
                for k in range(wide):
                    if h < PARTS - 1:
                        lanes = slice((c * wide + k) * LANES, (c * wide + k + 1) * LANES)
                        col_m[:, lanes], col_p[:, lanes] = tops[k], accs[k]
                    else:
                        full = jnp.max(tops[k], axis=0, keepdims=True)
                        tot = jnp.sum(accs[k] * jnp.exp2(tops[k] - full), axis=0, keepdims=True)
                        b_loc[step, c, k : k + 1, :] = full + jnp.log2(tot)
                if h == PARTS - 1:
                    for o, k in row_peers:
                        copy(
                            b_loc.at[step, c], b_all.at[step, c, row],
                            s_b.at[step], r_b.at[step, c], row_peer(o, k),
                        ).start()

    def receive_b(step, c):
        b_all[step, c, row] = b_loc[step, c]
        got = b_all.at[step, c, 0 : NR - 1]
        copy(got, got, s_b.at[step], r_b.at[step, c], peers[0]).wait_recv()
        pot = math.log2(n_src_total) - lse2([b_all[step, c, i] for i in range(NR)])
        part = slice(c * (ntb // PARTS), (c + 1) * (ntb // PARTS))
        gpot[part, :] = pot
        if step == ITERS - 1:
            g_out[part, :] = (pot + ny[part, :]) * UNSCALE

    first_row_pass()
    build_map_operand()
    for step in range(ITERS):
        if step > 0:
            later_row_pass(step)
        col_pass(step)
    for c in range(PARTS):
        receive_b(ITERS - 1, c)

    half = d // 2
    tail = half + 8
    order = sorted(range(NZ), key=lambda o: -hops(o, NZ))
    tops_of = [None] * NZ
    partner = col_peer(0, 1)

    def weights(t):
        base = pl.multiple_of((z + order[t]) % NZ * LANES, LANES)
        tops = []
        for q in range(LANES // 16):
            rows = pl.ds(pl.multiple_of(base + q * 16, 16), 16)
            ts = [
                score[rows, k * LANES : (k + 1) * LANES] + gpot[k : k + 1, :] for k in range(ntb)
            ]
            top = jnp.max(tree(jnp.maximum, ts), axis=1, keepdims=True)
            for k, v in enumerate(ts):
                w = jnp.exp2(v - top)
                w1 = w.astype(jnp.bfloat16)
                lanes = slice(k * LANES, (k + 1) * LANES)
                wbuf[t % 2, q * 16 : (q + 1) * 16, lanes] = w1
                wbuf[t % 2, LANES + q * 16 : LANES + (q + 1) * 16, lanes] = (
                    w - w1.astype(jnp.float32)
                ).astype(jnp.bfloat16)
            tops.append(jnp.broadcast_to(top, (16, LANES)))
        tops_of[t] = jnp.concatenate(tops, axis=0)

    def pair_copy(t):
        return copy(c_give.at[t], c_pair.at[t], s_p.at[0], r_p.at[t], partner)

    def product(t):
        both = jnp.dot(wbuf[t % 2], yt[...], preferred_element_type=jnp.float32)
        res = both[:LANES] + both[LANES:]
        lo = res[:, :LANES].T
        hi = jnp.where(lane == d + 1, tops_of[t], res[:, LANES:]).T
        num = lo[:d] + lo[d:] + hi[:d]
        c_mine[t, 0:half, :] = jnp.where(core == 0, num[:half], num[half:])
        c_give[t, 0:half, :] = jnp.where(core == 0, num[half:], num[:half])
        c_mine[t, half:tail, :] = hi[d : d + 8]
        c_give[t, half:tail, :] = hi[d : d + 8]
        pair_copy(t).start()

    def merge(parts):
        tops = [p[half + 1 : half + 2, :] for p in parts]
        top = tree(jnp.maximum, tops)
        tot = tree(jnp.add, [p[: half + 1, :] * jnp.exp2(v - top) for p, v in zip(parts, tops)])
        return tot, top

    def pair_merge(t):
        pair_copy(t).wait_recv()
        mine, other = c_mine[t], c_pair[t]
        tot, top = merge([jnp.where(core == 0, mine, other), jnp.where(core == 0, other, mine)])
        rest = jnp.broadcast_to(top, (7, LANES))
        if order[t] == 0:
            c_in[z, 0 : half + 1, :] = tot
            c_in[z, half + 1 : tail, :] = rest
        else:
            c_sum[t, 0 : half + 1, :] = tot
            c_sum[t, half + 1 : tail, :] = rest
            copy(c_sum.at[t], c_in.at[z], s_c.at[0], r_c.at[0], col_peer(order[t], 0)).start()

    weights(0)
    for t in range(NZ):
        if t + 1 < NZ:
            weights(t + 1)
        product(t)
        if t > 1:
            pair_merge(t - 2)
    pair_merge(NZ - 2)
    pair_merge(NZ - 1)
    got = c_in.at[0 : NZ - 1]
    c_whole = copy(got, got, s_c.at[0], r_c.at[0], peers[0])
    c_whole.wait_recv()
    tot, _ = merge([c_in[i] for i in range(NZ)])
    c_res[...] = tot[:half] / tot[half : half + 1]

    def gather_copy(o, k):
        return copy(c_res, c_all.at[core, z], s_g.at[0], r_g.at[o, k], col_peer(o, k))

    def relay_copy(o):
        piece = c_all.at[core, (z + NZ - o) % NZ]
        return copy(piece, piece, s_g.at[0], r_g.at[o, 1], partner)

    direct = NZ // 2
    for o in order[:-1]:
        gather_copy(o, 0).start()
        if o == direct:
            gather_copy(o, 1).start()
    gather_copy(0, 1).start()
    c_all[core, z] = c_res[...]
    for o in order[::-1][1:-1]:
        gather_copy(o, 0).wait_recv()
        relay_copy(o).start()

    for step in range(ITERS):
        a_got, b_got = a_all.at[step, :, 0 : NC - 1], b_all.at[step, :, 0 : NR - 1]
        copy(a_got, a_got, s_a.at[step], r_a.at[step, 0], peers[0]).wait_send()
        copy(b_got, b_got, s_b.at[step], r_b.at[step, 0], peers[0]).wait_send()
    copy(c_give, c_give, s_p.at[0], r_p.at[0], partner).wait_send()
    c_whole.wait_send()
    gather_copy(direct, 0).wait_recv()
    for o in range(NZ):
        gather_copy(o, 1).wait_recv()
    for k in range(2):
        for i in range(NZ):
            m_out[k * half : (k + 1) * half, i * LANES : (i + 1) * LANES] = c_all[k, i]
    flat = c_all.at[0, 0 : NZ - 1]
    copy(c_all.at[0], c_all.at[0], s_g.at[0], r_g.at[0, 0], partner).wait_send()
    copy(flat, flat, s_g.at[0], r_g.at[0, 0], partner).wait_send()


def solution(mesh):
    nrow, ncol = mesh.shape["row"], mesh.shape["col"]

    def shards(source, target):
        d, ns = source.shape
        nt = target.shape[1]
        nsb, ntb = ns // LANES, nt // LANES
        half = d // 2
        f32, bf16 = jnp.float32, jnp.bfloat16
        vmem = pltpu.VMEM
        dma = pltpu.SemaphoreType.DMA
        f, g, m = pl.pallas_call(
            functools.partial(kernel, ns * nrow, nt * ncol),
            out_shape=(
                jax.ShapeDtypeStruct((nsb, LANES), f32),
                jax.ShapeDtypeStruct((ntb, LANES), f32),
                jax.ShapeDtypeStruct((d, ns), f32),
            ),
            in_specs=[pl.BlockSpec(memory_space=pltpu.HBM)] * 2,
            out_specs=(pl.BlockSpec(memory_space=vmem),) * 3,
            scratch_shapes=[
                vmem((d, ns), f32),
                vmem((d, nt), f32),
                vmem((ns, 6 * d), bf16),
                vmem((6 * d, nt), bf16),
                vmem((nt, 2 * LANES), bf16),
                vmem((ns, nt), f32),
                vmem((nsb, LANES), f32),
                vmem((ntb, LANES), f32),
                vmem((ntb, LANES), f32),
                vmem((ns, LANES), f32),
                vmem((ns, LANES), f32),
                vmem((ns, LANES), f32),
                vmem((8, nt), f32),
                vmem((8, nt), f32),
                vmem((ITERS, PARTS, nsb // PARTS, LANES), f32),
                vmem((ITERS, PARTS, NC, nsb // PARTS, LANES), f32),
                vmem((ITERS, PARTS, ntb // PARTS, LANES), f32),
                vmem((ITERS, PARTS, NR, ntb // PARTS, LANES), f32),
                vmem((2, 2 * LANES, nt), bf16),
                vmem((NZ, half + 8, LANES), f32),
                vmem((NZ, half + 8, LANES), f32),
                vmem((NZ, half + 8, LANES), f32),
                vmem((NZ, half + 8, LANES), f32),
                vmem((NZ, half + 8, LANES), f32),
                vmem((half, LANES), f32),
                vmem((2, NZ, half, LANES), f32),
                dma((2,)),
                dma((ITERS,)),
                dma((ITERS, PARTS)),
                dma((ITERS,)),
                dma((ITERS, PARTS)),
                dma((1,)),
                dma((NZ,)),
                dma((1,)),
                dma((1,)),
                dma((1,)),
                dma((NZ, 2)),
            ],
            compiler_params=pltpu.CompilerParams(
                collective_id=0, has_side_effects=True, vmem_limit_bytes=40 * 2**20
            ),
            name="sinkhorn",
        )(source, target)
        return f.reshape(ns), g.reshape(nt), m

    return jax.shard_map(
        shards,
        mesh=mesh,
        in_specs=(P(None, "row"), P(None, "col")),
        out_specs=(P("row"), P("col"), P(None, "row")),
        check_vma=False,
    )
```

```python
import functools
import math

import jax
import jax.numpy as jnp
from jax import lax
from jax.experimental import pallas as pl
from jax.experimental.pallas import tpu as pltpu
from jax.sharding import PartitionSpec as P

MESH = pl.DeviceIdType.MESH
ITERS = 2
EPSILON = 0.005
SCALE = 1.0 / (EPSILON * math.log(2.0))
UNSCALE = EPSILON * math.log(2.0)
LANES = 128
NZ, NX, NY = 8, 4, 8
NC, NR = 2 * NZ, NX * NY
VMEM_GRANT = 56_150_000
PARTS = 2


def normalize(points):
    total = jnp.sum(points * points, axis=0, keepdims=True)
    return points / jnp.sqrt(total + 1e-06)


def split3(a):
    a1 = a.astype(jnp.bfloat16)
    r = a - a1.astype(jnp.float32)
    a2 = r.astype(jnp.bfloat16)
    a3 = (r - a2.astype(jnp.float32)).astype(jnp.bfloat16)
    return a1, a2, a3


def tree(op, xs):
    xs = list(xs)
    while len(xs) > 1:
        xs = [op(xs[i], xs[i + 1]) if i + 1 < len(xs) else xs[i] for i in range(0, len(xs), 2)]
    return xs[0]


def lse2(xs):
    top = tree(jnp.maximum, xs)
    return top + jnp.log2(tree(jnp.add, [jnp.exp2(x - top) for x in xs]))


def hops(o, n):
    return min(o, n - o)


def kernel(
    n_src_total,
    n_tgt_total,
    src_hbm,
    tgt_hbm,
    f_out,
    g_out,
    m_out,
    src,
    tgt,
    xk,
    yk,
    yt,
    yv,
    score,
    plan,
    halves,
    m_acc,
    nx,
    ny,
    fpot,
    gpot,
    fcol,
    part_m,
    part_p,
    col_m,
    col_p,
    a_loc,
    a_all,
    b_loc,
    b_all,
    c_mine,
    c_give,
    c_pair,
    c_sum,
    c_in,
    c_res,
    c_all,
    load,
    s_a,
    r_a,
    s_b,
    r_b,
    s_p,
    r_p,
    s_c,
    r_c,
    s_g,
    r_g,
):
    d, ns = src.shape
    nt = tgt.shape[1]
    nsb, ntb = ns // LANES, nt // LANES
    row, col = lax.axis_index("row"), lax.axis_index("col")
    y, x = row // NX, row % NX
    z, core = col // 2, col % 2

    load_src = pltpu.make_async_copy(src_hbm, src, load.at[0])
    load_tgt = pltpu.make_async_copy(tgt_hbm, tgt, load.at[1])
    load_src.start()
    load_tgt.start()

    col_peers = [(o, k) for o in range(NZ) for k in range(2) if (o, k) != (0, 0)]
    col_peers.sort(key=lambda p: -hops(p[0], NZ))
    row_peers = [(o, k) for o in range(NY) for k in range(NX) if (o, k) != (0, 0)]
    row_peers.sort(key=lambda p: -hops(p[0], NY) - hops(p[1], NX))

    def col_peer(o, k):
        return (row, ((z + o) % NZ) * 2 + (core + k) % 2)

    def row_peer(o, k):
        return (((y + o) % NY) * NX + (x + k) % NX, col)

    peers = [col_peer(*p) for p in col_peers] + [row_peer(*p) for p in row_peers]
    barrier = pltpu.get_barrier_semaphore()
    for peer in peers:
        pl.semaphore_signal(barrier, inc=1, device_id=peer, device_id_type=MESH)

    def copy(src_ref, dst_ref, send, recv, peer):
        return pltpu.make_async_remote_copy(
            src_ref=src_ref, dst_ref=dst_ref, send_sem=send, recv_sem=recv,
            device_id=peer, device_id_type=MESH,
        )

    load_src.wait()
    xs = normalize(src[...])
    nx_row = jnp.sum(xs * xs, axis=0, keepdims=True) * SCALE
    for b in range(nsb):
        nx[b : b + 1, :] = nx_row[:, b * LANES : (b + 1) * LANES]
    xs = xs * (2.0 * SCALE)
    first = lax.broadcasted_iota(jnp.int32, (LANES, LANES), 1) < d
    lane = lax.broadcasted_iota(jnp.int32, (LANES, LANES), 1)
    for b in range(nsb):
        blk = xs[:, b * LANES : (b + 1) * LANES]
        both = jnp.concatenate([blk, blk], axis=0).T
        x1 = both.astype(jnp.bfloat16).astype(jnp.float32)
        r = both - x1
        x2 = r.astype(jnp.bfloat16).astype(jnp.float32)
        rows = pl.ds(b * LANES, LANES)
        xk[rows, 0:128] = x1.astype(jnp.bfloat16)
        xk[rows, 128:256] = x2.astype(jnp.bfloat16)
        xk[rows, 256:384] = jnp.where(first, x1, r - x2).astype(jnp.bfloat16)
    load_tgt.wait()
    ys = normalize(tgt[...])
    tgt[...] = ys
    ny_row = jnp.sum(ys * ys, axis=0, keepdims=True) * SCALE
    for b in range(ntb):
        ny[b : b + 1, :] = ny_row[:, b * LANES : (b + 1) * LANES]
    y1, y2, y3 = split3(ys)
    for i, part in enumerate((y1, y2, y1, y2, y3, y1)):
        yk[i * d : (i + 1) * d, :] = part
    gpot[...] = -ny[...]

    def build_map_operand():
        for b in range(ntb):
            blk = tgt[:, b * LANES : (b + 1) * LANES]
            yt[b * LANES : (b + 1) * LANES, :] = jnp.concatenate(
                [blk, jnp.ones((LANES - d, LANES), jnp.float32)], axis=0
            ).T

    def score_tiles(c):
        rows = slice(c * 256, (c + 1) * 256)
        for n in range(nt // 256):
            lanes = slice(n * 256, (n + 1) * 256)

            def tile():
                score[rows, lanes] = jnp.dot(
                    xk[rows, :], yk[:, lanes], preferred_element_type=jnp.float32
                )

            yield tile

    def row_group(base, size):
        rows = pl.ds(base, size)
        ts = [score[rows, k * LANES : (k + 1) * LANES] + gpot[k : k + 1, :] for k in range(ntb)]
        top = tree(jnp.maximum, ts)
        part_m[rows, :] = top
        part_p[rows, :] = tree(jnp.add, [jnp.exp2(t - top) for t in ts])

    def plan_group(base, size, lo, hi):
        rows = pl.ds(base, size)
        pot = fcol[rows, :]
        ps = []
        for k in range(lo, hi):
            lanes = slice(k * LANES, (k + 1) * LANES)
            p = jnp.exp2((score[rows, lanes] + pot) + gpot[k : k + 1, :])
            plan[rows, lanes] = p
            ps.append(p)
        tot = tree(jnp.add, ps)
        part_p[rows, :] = tot if lo == 0 else tot + part_p[rows, :]

    def send_rows(step, c):
        for i in range(nsb // PARTS):
            b = c * (nsb // PARTS) + i
            pt = part_p[b * LANES : (b + 1) * LANES, :].T
            if step == 0:
                mt = part_m[b * LANES : (b + 1) * LANES, :].T
                top = jnp.max(mt, axis=0, keepdims=True)
                tot = jnp.sum(pt * jnp.exp2(mt - top), axis=0, keepdims=True)
                a_loc[step, c, i : i + 1, :] = top + jnp.log2(tot)
            else:
                a_loc[step, c, i : i + 1, :] = jnp.sum(pt, axis=0, keepdims=True)
        if step == 0 and c == 0:
            pl.semaphore_wait(barrier, len(peers))
        for o, k in col_peers:
            copy(
                a_loc.at[step, c], a_all.at[step, c, col],
                s_a.at[step], r_a.at[step, c], col_peer(o, k),
            ).start()

    def first_row_pass():
        count = ns // 256
        for c in range(count + 1):
            tiles = score_tiles(c) if c < count else [lambda: None] * (nt // 256)
            for n, tile in enumerate(tiles):
                tile()
                if c > 0:
                    for q in range(2):
                        row_group((c - 1) * 256 + n * 32 + q * 16, 16)
            if c > 0 and c % (count // PARTS) == 0:
                send_rows(0, c // (count // PARTS) - 1)

    def later_row_pass(step):
        wide = ntb // PARTS
        for c in range(PARTS):
            receive_b(step - 1, c)
            size = ns // PARTS
            for h in range(PARTS):

                def group(q, _):
                    base = pl.multiple_of(h * size + q * 32, 32)
                    plan_group(base, 32, c * wide, (c + 1) * wide)
                    return 0

                lax.fori_loop(0, size // 32, group, 0, unroll=8)
                if c == PARTS - 1:
                    send_rows(step, h)

    def receive_a(step, c):
        a_all[step, c, col] = a_loc[step, c]
        got = a_all.at[step, c, 0 : NC - 1]
        copy(got, got, s_a.at[step], r_a.at[step, c], peers[0]).wait_recv()
        size = nsb // PARTS
        part = slice(c * size, (c + 1) * size)
        if step == 0:
            pot = math.log2(n_tgt_total) - lse2([a_all[step, c, i] for i in range(NC)])
            fpot[part, :] = pot
        else:
            tot = tree(jnp.add, [a_all[step, c, i] for i in range(NC)])
            pot = (n_tgt_total / n_src_total) / tot
            f_out[part, :] = (fpot[part, :] + jnp.log2(pot) + nx[part, :]) * UNSCALE
        for i in range(size):
            b = c * size + i
            fcol[b * LANES : (b + 1) * LANES, :] = jnp.broadcast_to(
                pot[i : i + 1, :], (LANES, LANES)
            ).T

    def col_pass(step):
        wide = ntb // PARTS
        size = ns // PARTS
        for h in range(PARTS):
            receive_a(step, h)
            for c in range(PARTS):
                tops, accs = [None] * wide, [None] * wide
                if h > 0:
                    for k in range(wide):
                        lanes = slice((c * wide + k) * LANES, (c * wide + k + 1) * LANES)
                        tops[k], accs[k] = col_m[:, lanes], col_p[:, lanes]
                for b in range(size // 64):
                    for k in range(wide):
                        lanes = slice((c * wide + k) * LANES, (c * wide + k + 1) * LANES)
                        rows = slice(h * size + b * 64, h * size + (b + 1) * 64)
                        ts = (score[rows, lanes] + fcol[rows, :]).reshape(8, 8, LANES)
                        new = jnp.max(ts, axis=0)
                        if tops[k] is not None:
                            new = jnp.maximum(new, tops[k])
                        add = jnp.sum(jnp.exp2(ts - new[None]), axis=0)
                        if tops[k] is not None:
                            add += accs[k] * jnp.exp2(tops[k] - new)
                        tops[k], accs[k] = new, add
                for k in range(wide):
                    if h < PARTS - 1:
                        lanes = slice((c * wide + k) * LANES, (c * wide + k + 1) * LANES)
                        col_m[:, lanes], col_p[:, lanes] = tops[k], accs[k]
                    else:
                        full = jnp.max(tops[k], axis=0, keepdims=True)
                        tot = jnp.sum(accs[k] * jnp.exp2(tops[k] - full), axis=0, keepdims=True)
                        b_loc[step, c, k : k + 1, :] = full + jnp.log2(tot)
                if h == PARTS - 1:
                    send_cols(step, c)

    def plan_col_pass(step):
        wide = ntb // PARTS
        size = ns // PARTS
        for h in range(PARTS):
            receive_a(step, h)
            for c in range(PARTS):
                accs = [None] * wide
                for b in range(size // 64):
                    rows = slice(h * size + b * 64, h * size + (b + 1) * 64)
                    for k in range(wide):
                        lanes = slice((c * wide + k) * LANES, (c * wide + k + 1) * LANES)
                        ps = (plan[rows, lanes] * fcol[rows, :]).reshape(8, 8, LANES)
                        add = jnp.sum(ps, axis=0)
                        accs[k] = add if accs[k] is None else accs[k] + add
                for k in range(wide):
                    lanes = slice((c * wide + k) * LANES, (c * wide + k + 1) * LANES)
                    if h > 0:
                        accs[k] += col_p[:, lanes]
                    if h < PARTS - 1:
                        col_p[:, lanes] = accs[k]
                    else:
                        b_loc[step, c, k : k + 1, :] = jnp.sum(accs[k], axis=0, keepdims=True)
                if h == PARTS - 1:
                    send_cols(step, c)

    def send_cols(step, c):
        for o, k in row_peers:
            copy(
                b_loc.at[step, c], b_all.at[step, c, row],
                s_b.at[step], r_b.at[step, c], row_peer(o, k),
            ).start()

    def receive_b(step, c):
        b_all[step, c, row] = b_loc[step, c]
        got = b_all.at[step, c, 0 : NR - 1]
        copy(got, got, s_b.at[step], r_b.at[step, c], peers[0]).wait_recv()
        part = slice(c * (ntb // PARTS), (c + 1) * (ntb // PARTS))
        if step == 0:
            gpot[part, :] = -lse2([b_all[step, c, i] for i in range(NR)])
        else:
            fac = 1.0 / tree(jnp.add, [b_all[step, c, i] for i in range(NR)])
            g_out[part, :] = (
                gpot[part, :] + (jnp.log2(fac) + math.log2(n_src_total)) + ny[part, :]
            ) * UNSCALE
            for i in range(ntb // PARTS):
                b = c * (ntb // PARTS) + i
                rows = slice(b * LANES, (b + 1) * LANES)
                val = yt[rows, :] * jnp.broadcast_to(fac[i : i + 1, :], (LANES, LANES)).T
                v1 = val.astype(jnp.bfloat16)
                yv[rows, 0:LANES] = v1
                yv[rows, LANES : 2 * LANES] = (val - v1.astype(jnp.float32)).astype(jnp.bfloat16)

    order = sorted(range(NZ), key=lambda o: -hops(o, NZ))

    def split_plan():
        for t in range(NZ):
            base = pl.multiple_of((z + order[t]) % NZ * LANES, LANES)
            for q in range(LANES // 16):
                p = plan[pl.ds(pl.multiple_of(base + q * 16, 16), 16), :]
                p1 = p.astype(jnp.bfloat16)
                halves[t, q * 16 : (q + 1) * 16, :] = p1
                halves[t, LANES + q * 16 : LANES + (q + 1) * 16, :] = (
                    p - p1.astype(jnp.float32)
                ).astype(jnp.bfloat16)

    first_row_pass()
    build_map_operand()
    col_pass(0)
    later_row_pass(1)
    plan_col_pass(1)
    split_plan()

    half = d // 2
    partner = col_peer(0, 1)

    def product(t, c):
        part = slice(c * (nt // PARTS), (c + 1) * (nt // PARTS))
        both = jnp.dot(halves[t, :, part], yv[part, :], preferred_element_type=jnp.float32)
        both = both[:LANES] + both[LANES:]
        return both[:, :LANES] + both[:, LANES:]

    for c in range(PARTS - 1):
        receive_b(1, c)
        for t in range(NZ):
            res = product(t, c)
            m_acc[t] = res if c == 0 else m_acc[t] + res
    receive_b(1, PARTS - 1)

    def pair_copy(t):
        return copy(c_give.at[t], c_pair.at[t], s_p.at[0], r_p.at[t], partner)

    def finish_block(t):
        res = (m_acc[t] + product(t, PARTS - 1)).T
        c_mine[t, 0:half, :] = jnp.where(core == 0, res[:half], res[half:d])
        c_give[t, 0:half, :] = jnp.where(core == 0, res[half:d], res[:half])
        c_mine[t, half : half + 1, :] = res[d : d + 1]
        c_give[t, half : half + 1, :] = res[d : d + 1]
        pair_copy(t).start()

    def pair_merge(t):
        pair_copy(t).wait_recv()
        if order[t] == 0:
            c_in[z] = c_mine[t] + c_pair[t]
        else:
            c_sum[t] = c_mine[t] + c_pair[t]
            copy(c_sum.at[t], c_in.at[z], s_c.at[0], r_c.at[0], col_peer(order[t], 0)).start()

    lag = 4
    for t in range(NZ):
        finish_block(t)
        if t >= lag:
            pair_merge(t - lag)
    for t in range(NZ - lag, NZ):
        pair_merge(t)
    got = c_in.at[0 : NZ - 1]
    c_whole = copy(got, got, s_c.at[0], r_c.at[0], peers[0])
    c_whole.wait_recv()
    tot = tree(jnp.add, [c_in[i] for i in range(NZ)])
    c_res[...] = tot[:half] / tot[half : half + 1]

    def gather_copy(o, k):
        return copy(c_res, c_all.at[core, z], s_g.at[0], r_g.at[o, k], col_peer(o, k))

    def relay_copy(o):
        piece = c_all.at[core, (z + NZ - o) % NZ]
        return copy(piece, piece, s_g.at[0], r_g.at[o, 1], partner)

    direct = NZ // 2
    for o in order[:-1]:
        gather_copy(o, 0).start()
        if o == direct:
            gather_copy(o, 1).start()
    gather_copy(0, 1).start()
    c_all[core, z] = c_res[...]
    for o in order[::-1][1:-1]:
        gather_copy(o, 0).wait_recv()
        relay_copy(o).start()

    for step in range(ITERS):
        a_got, b_got = a_all.at[step, :, 0 : NC - 1], b_all.at[step, :, 0 : NR - 1]
        copy(a_got, a_got, s_a.at[step], r_a.at[step, 0], peers[0]).wait_send()
        copy(b_got, b_got, s_b.at[step], r_b.at[step, 0], peers[0]).wait_send()
    copy(c_give, c_give, s_p.at[0], r_p.at[0], partner).wait_send()
    c_whole.wait_send()
    gather_copy(direct, 0).wait_recv()
    for o in range(NZ):
        gather_copy(o, 1).wait_recv()
    for k in range(2):
        for i in range(NZ):
            m_out[k * half : (k + 1) * half, i * LANES : (i + 1) * LANES] = c_all[k, i]
    flat = c_all.at[0, 0 : NZ - 1]
    copy(c_all.at[0], c_all.at[0], s_g.at[0], r_g.at[0, 0], partner).wait_send()
    copy(flat, flat, s_g.at[0], r_g.at[0, 0], partner).wait_send()


def write_kernel(f, g, m, f_out, g_out, m_out, sems):
    copies = [
        pltpu.make_async_copy(a, b, sems.at[i])
        for i, (a, b) in enumerate(((m, m_out), (g, g_out), (f, f_out)))
    ]
    for c in copies:
        c.start()
    for c in copies:
        c.wait()


def solution(mesh):
    nrow, ncol = mesh.shape["row"], mesh.shape["col"]

    def shards(source, target):
        d, ns = source.shape
        nt = target.shape[1]
        nsb, ntb = ns // LANES, nt // LANES
        half = d // 2
        f32, bf16 = jnp.float32, jnp.bfloat16
        vmem = pltpu.VMEM
        dma = pltpu.SemaphoreType.DMA
        f, g, m = pl.pallas_call(
            functools.partial(kernel, ns * nrow, nt * ncol),
            out_shape=(
                jax.ShapeDtypeStruct((nsb, LANES), f32),
                jax.ShapeDtypeStruct((ntb, LANES), f32),
                jax.ShapeDtypeStruct((d, ns), f32),
            ),
            in_specs=[pl.BlockSpec(memory_space=pltpu.HBM)] * 2,
            out_specs=(pl.BlockSpec(memory_space=vmem),) * 3,
            scratch_shapes=[
                vmem((d, ns), f32),
                vmem((d, nt), f32),
                vmem((ns, 6 * d), bf16),
                vmem((6 * d, nt), bf16),
                vmem((nt, LANES), f32),
                vmem((nt, 2 * LANES), bf16),
                vmem((ns, nt), f32),
                vmem((ns, nt), f32),
                vmem((NZ, 2 * LANES, nt), bf16),
                vmem((NZ, LANES, LANES), f32),
                vmem((nsb, LANES), f32),
                vmem((ntb, LANES), f32),
                vmem((nsb, LANES), f32),
                vmem((ntb, LANES), f32),
                vmem((ns, LANES), f32),
                vmem((ns, LANES), f32),
                vmem((ns, LANES), f32),
                vmem((8, nt), f32),
                vmem((8, nt), f32),
                vmem((ITERS, PARTS, nsb // PARTS, LANES), f32),
                vmem((ITERS, PARTS, NC, nsb // PARTS, LANES), f32),
                vmem((ITERS, PARTS, ntb // PARTS, LANES), f32),
                vmem((ITERS, PARTS, NR, ntb // PARTS, LANES), f32),
                vmem((NZ, half + 1, LANES), f32),
                vmem((NZ, half + 1, LANES), f32),
                vmem((NZ, half + 1, LANES), f32),
                vmem((NZ, half + 1, LANES), f32),
                vmem((NZ, half + 1, LANES), f32),
                vmem((half, LANES), f32),
                vmem((2, NZ, half, LANES), f32),
                dma((2,)),
                dma((ITERS,)),
                dma((ITERS, PARTS)),
                dma((ITERS,)),
                dma((ITERS, PARTS)),
                dma((1,)),
                dma((NZ,)),
                dma((1,)),
                dma((1,)),
                dma((1,)),
                dma((NZ, 2)),
            ],
            compiler_params=pltpu.CompilerParams(
                collective_id=0, has_side_effects=True, vmem_limit_bytes=VMEM_GRANT
            ),
            name="sinkhorn",
        )(source, target)
        f, g, m = pl.pallas_call(
            write_kernel,
            out_shape=(
                jax.ShapeDtypeStruct((nsb, LANES), f32),
                jax.ShapeDtypeStruct((ntb, LANES), f32),
                jax.ShapeDtypeStruct((d, ns), f32),
            ),
            in_specs=[pl.BlockSpec(memory_space=pl.ANY)] * 3,
            out_specs=(pl.BlockSpec(memory_space=pl.ANY),) * 3,
            scratch_shapes=[dma((3,))],
            compiler_params=pltpu.CompilerParams(vmem_limit_bytes=2**20),
            name="write_results",
        )(f, g, m)
        return f.reshape(ns), g.reshape(nt), m

    return jax.shard_map(
        shards,
        mesh=mesh,
        in_specs=(P(None, "row"), P(None, "col")),
        out_specs=(P("row"), P("col"), P(None, "row")),
        check_vma=False,
    )
```

```python
import functools
import math

import jax
import jax.numpy as jnp
from jax import lax
from jax.experimental import pallas as pl
from jax.experimental.pallas import tpu as pltpu
from jax.sharding import PartitionSpec as P

MESH = pl.DeviceIdType.MESH
ITERS = 2
EPSILON = 0.005
SCALE = 1.0 / (EPSILON * math.log(2.0))
UNSCALE = EPSILON * math.log(2.0)
LANES = 128
NZ, NX, NY = 8, 4, 8
NC, NR = 2 * NZ, NX * NY
VMEM_GRANT = 56_150_000
PARTS = 2


def normalize(points):
    total = jnp.sum(points * points, axis=0, keepdims=True)
    return points / jnp.sqrt(total + 1e-06)


def split3(a):
    a1 = a.astype(jnp.bfloat16)
    r = a - a1.astype(jnp.float32)
    a2 = r.astype(jnp.bfloat16)
    a3 = (r - a2.astype(jnp.float32)).astype(jnp.bfloat16)
    return a1, a2, a3


def tree(op, xs):
    xs = list(xs)
    while len(xs) > 1:
        xs = [op(xs[i], xs[i + 1]) if i + 1 < len(xs) else xs[i] for i in range(0, len(xs), 2)]
    return xs[0]


def lse2(xs):
    top = tree(jnp.maximum, xs)
    return top + jnp.log2(tree(jnp.add, [jnp.exp2(x - top) for x in xs]))


def hops(o, n):
    return min(o, n - o)


def kernel(
    n_src_total,
    n_tgt_total,
    src_hbm,
    tgt_hbm,
    f_out,
    g_out,
    m_out,
    src,
    tgt,
    xk,
    yk,
    yt,
    yv,
    score,
    plan,
    halves,
    m_acc,
    nx,
    ny,
    fpot,
    gpot,
    fcol,
    part_m,
    part_p,
    col_m,
    col_p,
    a_loc,
    a_all,
    b_loc,
    b_all,
    c_mine,
    c_give,
    c_pair,
    c_sum,
    c_in,
    c_res,
    c_all,
    load,
    s_a,
    r_a,
    s_b,
    r_b,
    s_p,
    r_p,
    s_c,
    r_c,
    s_g,
    r_g,
):
    d, ns = src.shape
    nt = tgt.shape[1]
    nsb, ntb = ns // LANES, nt // LANES
    row, col = lax.axis_index("row"), lax.axis_index("col")
    y, x = row // NX, row % NX
    z, core = col // 2, col % 2

    load_src = pltpu.make_async_copy(src_hbm, src, load.at[0])
    load_tgt = pltpu.make_async_copy(tgt_hbm, tgt, load.at[1])
    load_src.start()
    load_tgt.start()

    col_peers = [(o, k) for o in range(NZ) for k in range(2) if (o, k) != (0, 0)]
    col_peers.sort(key=lambda p: -hops(p[0], NZ))
    row_peers = [(o, k) for o in range(NY) for k in range(NX) if (o, k) != (0, 0)]
    row_peers.sort(key=lambda p: -hops(p[0], NY) - hops(p[1], NX))

    def col_peer(o, k):
        return (row, ((z + o) % NZ) * 2 + (core + k) % 2)

    def row_peer(o, k):
        return (((y + o) % NY) * NX + (x + k) % NX, col)

    col_ids = {p: col_peer(*p) for p in col_peers}
    row_ids = {p: row_peer(*p) for p in row_peers}
    peers = list(col_ids.values()) + list(row_ids.values())
    barrier = pltpu.get_barrier_semaphore()
    for peer in peers:
        pl.semaphore_signal(barrier, inc=1, device_id=peer, device_id_type=MESH)

    def copy(src_ref, dst_ref, send, recv, peer):
        return pltpu.make_async_remote_copy(
            src_ref=src_ref, dst_ref=dst_ref, send_sem=send, recv_sem=recv,
            device_id=peer, device_id_type=MESH,
        )

    load_src.wait()
    xs = normalize(src[...])
    nx_row = jnp.sum(xs * xs, axis=0, keepdims=True) * SCALE
    for b in range(nsb):
        nx[b : b + 1, :] = nx_row[:, b * LANES : (b + 1) * LANES]
    xs = xs * (2.0 * SCALE)
    first = lax.broadcasted_iota(jnp.int32, (LANES, LANES), 1) < d
    lane = lax.broadcasted_iota(jnp.int32, (LANES, LANES), 1)
    for b in range(nsb):
        blk = xs[:, b * LANES : (b + 1) * LANES]
        both = jnp.concatenate([blk, blk], axis=0).T
        x1 = both.astype(jnp.bfloat16).astype(jnp.float32)
        r = both - x1
        x2 = r.astype(jnp.bfloat16).astype(jnp.float32)
        rows = pl.ds(b * LANES, LANES)
        xk[rows, 0:128] = x1.astype(jnp.bfloat16)
        xk[rows, 128:256] = x2.astype(jnp.bfloat16)
        xk[rows, 256:384] = jnp.where(first, x1, r - x2).astype(jnp.bfloat16)
    load_tgt.wait()
    ys = normalize(tgt[...])
    tgt[...] = ys
    ny_row = jnp.sum(ys * ys, axis=0, keepdims=True) * SCALE
    for b in range(ntb):
        ny[b : b + 1, :] = ny_row[:, b * LANES : (b + 1) * LANES]
    y1, y2, y3 = split3(ys)
    for i, part in enumerate((y1, y2, y1, y2, y3, y1)):
        yk[i * d : (i + 1) * d, :] = part
    gpot[...] = -ny[...]

    def build_map_operand():
        for b in range(ntb):
            blk = tgt[:, b * LANES : (b + 1) * LANES]
            yt[b * LANES : (b + 1) * LANES, :] = jnp.concatenate(
                [blk, jnp.ones((LANES - d, LANES), jnp.float32)], axis=0
            ).T

    def score_tiles(c):
        rows = slice(c * 256, (c + 1) * 256)
        for n in range(nt // 256):
            lanes = slice(n * 256, (n + 1) * 256)

            def tile():
                score[rows, lanes] = jnp.dot(
                    xk[rows, :], yk[:, lanes], preferred_element_type=jnp.float32
                )

            yield tile

    def row_group(base, size):
        rows = pl.ds(base, size)
        ts = [score[rows, k * LANES : (k + 1) * LANES] + gpot[k : k + 1, :] for k in range(ntb)]
        top = tree(jnp.maximum, ts)
        part_m[rows, :] = top
        part_p[rows, :] = tree(jnp.add, [jnp.exp2(t - top) for t in ts])

    def plan_group(base, size, lo, hi):
        rows = pl.ds(base, size)
        pot = fcol[rows, :]
        ps = []
        for k in range(lo, hi):
            lanes = slice(k * LANES, (k + 1) * LANES)
            p = jnp.exp2((score[rows, lanes] + pot) + gpot[k : k + 1, :])
            plan[rows, lanes] = p
            ps.append(p)
        tot = tree(jnp.add, ps)
        part_p[rows, :] = tot if lo == 0 else tot + part_p[rows, :]

    def send_rows(step, c):
        for i in range(nsb // PARTS):
            b = c * (nsb // PARTS) + i
            pt = part_p[b * LANES : (b + 1) * LANES, :].T
            if step == 0:
                mt = part_m[b * LANES : (b + 1) * LANES, :].T
                top = jnp.max(mt, axis=0, keepdims=True)
                tot = jnp.sum(pt * jnp.exp2(mt - top), axis=0, keepdims=True)
                a_loc[step, c, i : i + 1, :] = top + jnp.log2(tot)
            else:
                a_loc[step, c, i : i + 1, :] = jnp.sum(pt, axis=0, keepdims=True)
        if step == 0 and c == 0:
            pl.semaphore_wait(barrier, len(peers))
        for o, k in col_peers:
            copy(
                a_loc.at[step, c], a_all.at[step, c, col],
                s_a.at[step], r_a.at[step, c], col_peer(o, k),
            ).start()

    def first_row_pass():
        count = ns // 256
        for c in range(count + 1):
            tiles = score_tiles(c) if c < count else [lambda: None] * (nt // 256)
            for n, tile in enumerate(tiles):
                tile()
                if c > 0:
                    for q in range(2):
                        row_group((c - 1) * 256 + n * 32 + q * 16, 16)
            if c > 0 and c % (count // PARTS) == 0:
                send_rows(0, c // (count // PARTS) - 1)

    def later_row_pass(step):
        wide = ntb // PARTS
        for c in range(PARTS):
            receive_b(step - 1, c)
            size = ns // PARTS
            for h in range(PARTS):

                def group(q, _):
                    base = pl.multiple_of(h * size + q * 32, 32)
                    plan_group(base, 32, c * wide, (c + 1) * wide)
                    return 0

                lax.fori_loop(0, size // 32, group, 0, unroll=8)
                if c == PARTS - 1:
                    send_rows(step, h)

    def receive_a(step, c):
        a_all[step, c, col] = a_loc[step, c]
        got = a_all.at[step, c, 0 : NC - 1]
        copy(got, got, s_a.at[step], r_a.at[step, c], peers[0]).wait_recv()
        size = nsb // PARTS
        part = slice(c * size, (c + 1) * size)
        if step == 0:
            pot = math.log2(n_tgt_total) - lse2([a_all[step, c, i] for i in range(NC)])
            fpot[part, :] = pot
        else:
            tot = tree(jnp.add, [a_all[step, c, i] for i in range(NC)])
            pot = (n_tgt_total / n_src_total) / tot
            f_out[part, :] = (fpot[part, :] + jnp.log2(pot) + nx[part, :]) * UNSCALE
        for i in range(size):
            b = c * size + i
            fcol[b * LANES : (b + 1) * LANES, :] = jnp.broadcast_to(
                pot[i : i + 1, :], (LANES, LANES)
            ).T

    def col_pass(step):
        wide = ntb // PARTS
        size = ns // PARTS
        for h in range(PARTS):
            receive_a(step, h)
            for c in range(PARTS):
                tops, accs = [None] * wide, [None] * wide
                if h > 0:
                    for k in range(wide):
                        lanes = slice((c * wide + k) * LANES, (c * wide + k + 1) * LANES)
                        tops[k], accs[k] = col_m[:, lanes], col_p[:, lanes]
                for b in range(size // 64):
                    for k in range(wide):
                        lanes = slice((c * wide + k) * LANES, (c * wide + k + 1) * LANES)
                        rows = slice(h * size + b * 64, h * size + (b + 1) * 64)
                        ts = (score[rows, lanes] + fcol[rows, :]).reshape(8, 8, LANES)
                        new = jnp.max(ts, axis=0)
                        if tops[k] is not None:
                            new = jnp.maximum(new, tops[k])
                        add = jnp.sum(jnp.exp2(ts - new[None]), axis=0)
                        if tops[k] is not None:
                            add += accs[k] * jnp.exp2(tops[k] - new)
                        tops[k], accs[k] = new, add
                for k in range(wide):
                    if h < PARTS - 1:
                        lanes = slice((c * wide + k) * LANES, (c * wide + k + 1) * LANES)
                        col_m[:, lanes], col_p[:, lanes] = tops[k], accs[k]
                    else:
                        full = jnp.max(tops[k], axis=0, keepdims=True)
                        tot = jnp.sum(accs[k] * jnp.exp2(tops[k] - full), axis=0, keepdims=True)
                        b_loc[step, c, k : k + 1, :] = full + jnp.log2(tot)
                if h == PARTS - 1:
                    send_cols(step, c)

    def plan_col_pass(step):
        wide = ntb // PARTS
        size = ns // PARTS
        for h in range(PARTS):
            receive_a(step, h)
            for c in range(PARTS):
                accs = [None] * wide
                for b in range(size // 64):
                    rows = slice(h * size + b * 64, h * size + (b + 1) * 64)
                    for k in range(wide):
                        lanes = slice((c * wide + k) * LANES, (c * wide + k + 1) * LANES)
                        ps = (plan[rows, lanes] * fcol[rows, :]).reshape(8, 8, LANES)
                        add = jnp.sum(ps, axis=0)
                        accs[k] = add if accs[k] is None else accs[k] + add
                for k in range(wide):
                    lanes = slice((c * wide + k) * LANES, (c * wide + k + 1) * LANES)
                    if h > 0:
                        accs[k] += col_p[:, lanes]
                    if h < PARTS - 1:
                        col_p[:, lanes] = accs[k]
                    else:
                        b_loc[step, c, k : k + 1, :] = jnp.sum(accs[k], axis=0, keepdims=True)
                if h == PARTS - 1:
                    send_cols(step, c)

    def send_cols(step, c):
        for o, k in row_peers:
            copy(
                b_loc.at[step, c], b_all.at[step, c, row],
                s_b.at[step], r_b.at[step, c], row_ids[o, k],
            ).start()

    def receive_b(step, c):
        b_all[step, c, row] = b_loc[step, c]
        got = b_all.at[step, c, 0 : NR - 1]
        copy(got, got, s_b.at[step], r_b.at[step, c], peers[0]).wait_recv()
        part = slice(c * (ntb // PARTS), (c + 1) * (ntb // PARTS))
        if step == 0:
            gpot[part, :] = -lse2([b_all[step, c, i] for i in range(NR)])
        else:
            fac = 1.0 / tree(jnp.add, [b_all[step, c, i] for i in range(NR)])
            g_out[part, :] = (
                gpot[part, :] + (jnp.log2(fac) + math.log2(n_src_total)) + ny[part, :]
            ) * UNSCALE
            for i in range(ntb // PARTS):
                b = c * (ntb // PARTS) + i
                rows = slice(b * LANES, (b + 1) * LANES)
                val = yt[rows, :] * jnp.broadcast_to(fac[i : i + 1, :], (LANES, LANES)).T
                v1 = val.astype(jnp.bfloat16)
                yv[rows, 0:LANES] = v1
                yv[rows, LANES : 2 * LANES] = (val - v1.astype(jnp.float32)).astype(jnp.bfloat16)

    order = sorted(range(NZ), key=lambda o: -hops(o, NZ))

    def split_plan():
        for t in range(NZ):
            base = pl.multiple_of((z + order[t]) % NZ * LANES, LANES)
            for q in range(LANES // 16):
                p = plan[pl.ds(pl.multiple_of(base + q * 16, 16), 16), :]
                p1 = p.astype(jnp.bfloat16)
                at = t * 2 * LANES + q * 16
                halves[at : at + 16, :] = p1
                halves[at + LANES : at + LANES + 16, :] = (
                    p - p1.astype(jnp.float32)
                ).astype(jnp.bfloat16)

    first_row_pass()
    build_map_operand()
    col_pass(0)
    later_row_pass(1)
    plan_col_pass(1)
    split_plan()

    half = d // 2
    partner = col_peer(0, 1)

    def product(t, count, c):
        part = slice(c * (nt // PARTS), (c + 1) * (nt // PARTS))
        rows = slice(t * 2 * LANES, (t + count) * 2 * LANES)
        both = jnp.dot(halves[rows, part], yv[part, :], preferred_element_type=jnp.float32)
        both = both[:, :LANES] + both[:, LANES:]
        out = []
        for i in range(count):
            at = i * 2 * LANES
            out.append(both[at : at + LANES] + both[at + LANES : at + 2 * LANES])
        return out

    for c in range(PARTS - 1):
        receive_b(1, c)
        for t, res in enumerate(product(0, NZ, c)):
            m_acc[t] = res if c == 0 else m_acc[t] + res
    receive_b(1, PARTS - 1)

    GROUP = NZ // 2

    def pair_copy(g):
        part = pl.ds(g * GROUP, GROUP)
        return copy(c_give.at[part], c_pair.at[part], s_p.at[0], r_p.at[g], partner)

    def finish_group(g):
        for i, res in enumerate(product(g * GROUP, GROUP, PARTS - 1)):
            t = g * GROUP + i
            res = (m_acc[t] + res).T
            c_mine[t, 0:half, :] = jnp.where(core == 0, res[:half], res[half:d])
            c_give[t, 0:half, :] = jnp.where(core == 0, res[half:d], res[:half])
            c_mine[t, half : half + 1, :] = res[d : d + 1]
            c_give[t, half : half + 1, :] = res[d : d + 1]
        pair_copy(g).start()

    def merge_group(g):
        pair_copy(g).wait_recv()
        for t in range(g * GROUP, (g + 1) * GROUP):
            if order[t] == 0:
                c_in[z] = c_mine[t] + c_pair[t]
            else:
                c_sum[t] = c_mine[t] + c_pair[t]
        for t in range(g * GROUP, (g + 1) * GROUP):
            if order[t] != 0:
                copy(c_sum.at[t], c_in.at[z], s_c.at[0], r_c.at[0], col_peer(order[t], 0)).start()

    finish_group(0)
    finish_group(1)
    merge_group(0)
    merge_group(1)
    got = c_in.at[0 : NZ - 1]
    c_whole = copy(got, got, s_c.at[0], r_c.at[0], peers[0])
    c_whole.wait_recv()
    tot = tree(jnp.add, [c_in[i] for i in range(NZ)])
    c_res[...] = tot[:half] / tot[half : half + 1]

    def gather_copy(o, k):
        return copy(c_res, c_all.at[core, z], s_g.at[0], r_g.at[o, k], col_peer(o, k))

    def relay_copy(o):
        piece = c_all.at[core, (z + NZ - o) % NZ]
        return copy(piece, piece, s_g.at[0], r_g.at[o, 1], partner)

    direct = NZ // 2
    for o in order[:-1]:
        gather_copy(o, 0).start()
        if o == direct:
            gather_copy(o, 1).start()
    gather_copy(0, 1).start()
    c_all[core, z] = c_res[...]
    for o in order[::-1][1:-1]:
        gather_copy(o, 0).wait_recv()
        relay_copy(o).start()

    for step in range(ITERS):
        a_got, b_got = a_all.at[step, :, 0 : NC - 1], b_all.at[step, :, 0 : NR - 1]
        copy(a_got, a_got, s_a.at[step], r_a.at[step, 0], peers[0]).wait_send()
        copy(b_got, b_got, s_b.at[step], r_b.at[step, 0], peers[0]).wait_send()
    copy(c_give, c_give, s_p.at[0], r_p.at[0], partner).wait_send()
    c_whole.wait_send()
    gather_copy(direct, 0).wait_recv()
    for o in range(NZ):
        gather_copy(o, 1).wait_recv()
    for k in range(2):
        for i in range(NZ):
            m_out[k * half : (k + 1) * half, i * LANES : (i + 1) * LANES] = c_all[k, i]
    flat = c_all.at[0, 0 : NZ - 1]
    copy(c_all.at[0], c_all.at[0], s_g.at[0], r_g.at[0, 0], partner).wait_send()
    copy(flat, flat, s_g.at[0], r_g.at[0, 0], partner).wait_send()


def write_kernel(f, g, m, f_out, g_out, m_out, sems):
    copies = [
        pltpu.make_async_copy(a, b, sems.at[i])
        for i, (a, b) in enumerate(((m, m_out), (g, g_out), (f, f_out)))
    ]
    for c in copies:
        c.start()
    for c in copies:
        c.wait()


def solution(mesh):
    nrow, ncol = mesh.shape["row"], mesh.shape["col"]

    def shards(source, target):
        d, ns = source.shape
        nt = target.shape[1]
        nsb, ntb = ns // LANES, nt // LANES
        half = d // 2
        f32, bf16 = jnp.float32, jnp.bfloat16
        vmem = pltpu.VMEM
        dma = pltpu.SemaphoreType.DMA
        f, g, m = pl.pallas_call(
            functools.partial(kernel, ns * nrow, nt * ncol),
            out_shape=(
                jax.ShapeDtypeStruct((nsb, LANES), f32),
                jax.ShapeDtypeStruct((ntb, LANES), f32),
                jax.ShapeDtypeStruct((d, ns), f32),
            ),
            in_specs=[pl.BlockSpec(memory_space=pltpu.HBM)] * 2,
            out_specs=(pl.BlockSpec(memory_space=vmem),) * 3,
            scratch_shapes=[
                vmem((d, ns), f32),
                vmem((d, nt), f32),
                vmem((ns, 6 * d), bf16),
                vmem((6 * d, nt), bf16),
                vmem((nt, LANES), f32),
                vmem((nt, 2 * LANES), bf16),
                vmem((ns, nt), f32),
                vmem((ns, nt), f32),
                vmem((NZ * 2 * LANES, nt), bf16),
                vmem((NZ, LANES, LANES), f32),
                vmem((nsb, LANES), f32),
                vmem((ntb, LANES), f32),
                vmem((nsb, LANES), f32),
                vmem((ntb, LANES), f32),
                vmem((ns, LANES), f32),
                vmem((ns, LANES), f32),
                vmem((ns, LANES), f32),
                vmem((8, nt), f32),
                vmem((8, nt), f32),
                vmem((ITERS, PARTS, nsb // PARTS, LANES), f32),
                vmem((ITERS, PARTS, NC, nsb // PARTS, LANES), f32),
                vmem((ITERS, PARTS, ntb // PARTS, LANES), f32),
                vmem((ITERS, PARTS, NR, ntb // PARTS, LANES), f32),
                vmem((NZ, half + 1, LANES), f32),
                vmem((NZ, half + 1, LANES), f32),
                vmem((NZ, half + 1, LANES), f32),
                vmem((NZ, half + 1, LANES), f32),
                vmem((NZ, half + 1, LANES), f32),
                vmem((half, LANES), f32),
                vmem((2, NZ, half, LANES), f32),
                dma((2,)),
                dma((ITERS,)),
                dma((ITERS, PARTS)),
                dma((ITERS,)),
                dma((ITERS, PARTS)),
                dma((1,)),
                dma((NZ,)),
                dma((1,)),
                dma((1,)),
                dma((1,)),
                dma((NZ, 2)),
            ],
            compiler_params=pltpu.CompilerParams(
                collective_id=0, has_side_effects=True, vmem_limit_bytes=VMEM_GRANT
            ),
            name="sinkhorn",
        )(source, target)
        f, g, m = pl.pallas_call(
            write_kernel,
            out_shape=(
                jax.ShapeDtypeStruct((nsb, LANES), f32),
                jax.ShapeDtypeStruct((ntb, LANES), f32),
                jax.ShapeDtypeStruct((d, ns), f32),
            ),
            in_specs=[pl.BlockSpec(memory_space=pl.ANY)] * 3,
            out_specs=(pl.BlockSpec(memory_space=pl.ANY),) * 3,
            scratch_shapes=[dma((3,))],
            compiler_params=pltpu.CompilerParams(vmem_limit_bytes=2**20),
            name="write_results",
        )(f, g, m)
        return f.reshape(ns), g.reshape(nt), m

    return jax.shard_map(
        shards,
        mesh=mesh,
        in_specs=(P(None, "row"), P(None, "col")),
        out_specs=(P("row"), P("col"), P(None, "row")),
        check_vma=False,
    )
```

```python
import functools
import math

import jax
import jax.numpy as jnp
from jax import lax
from jax.experimental import pallas as pl
from jax.experimental.pallas import tpu as pltpu
from jax.sharding import PartitionSpec as P

MESH = pl.DeviceIdType.MESH
ITERS = 2
EPSILON = 0.005
SCALE = 1.0 / (EPSILON * math.log(2.0))
UNSCALE = EPSILON * math.log(2.0)
LANES = 128
NZ, NX, NY = 8, 4, 8
NC = 2 * NZ
VMEM_GRANT = 56_150_000
PARTS = 2


def normalize(points):
    total = jnp.sum(points * points, axis=0, keepdims=True)
    return points / jnp.sqrt(total + 1e-06)


def split3(a):
    a1 = a.astype(jnp.bfloat16)
    r = a - a1.astype(jnp.float32)
    a2 = r.astype(jnp.bfloat16)
    a3 = (r - a2.astype(jnp.float32)).astype(jnp.bfloat16)
    return a1, a2, a3


def tree(op, xs):
    xs = list(xs)
    while len(xs) > 1:
        xs = [op(xs[i], xs[i + 1]) if i + 1 < len(xs) else xs[i] for i in range(0, len(xs), 2)]
    return xs[0]


def lse2(xs):
    top = tree(jnp.maximum, xs)
    return top + jnp.log2(tree(jnp.add, [jnp.exp2(x - top) for x in xs]))


def hops(o, n):
    return min(o, n - o)


def kernel(
    n_src_total,
    n_tgt_total,
    src_hbm,
    tgt_hbm,
    f_out,
    g_out,
    m_out,
    src,
    tgt,
    xk,
    yk,
    yt,
    yv,
    score,
    plan,
    halves,
    m_acc,
    nx,
    ny,
    fpot,
    gpot,
    fcol,
    part_m,
    part_p,
    col_m,
    col_p,
    a_loc,
    a_all,
    b_loc,
    b_y,
    b_mid,
    b_x,
    c_mine,
    c_give,
    c_pair,
    c_sum,
    c_in,
    c_res,
    c_all,
    load,
    s_a,
    r_a,
    s_by,
    r_by,
    s_bx,
    r_bx,
    s_p,
    r_p,
    s_c,
    r_c,
    s_g,
    r_g,
):
    d, ns = src.shape
    nt = tgt.shape[1]
    nsb, ntb = ns // LANES, nt // LANES
    row, col = lax.axis_index("row"), lax.axis_index("col")
    y, x = row // NX, row % NX
    z, core = col // 2, col % 2

    load_src = pltpu.make_async_copy(src_hbm, src, load.at[0])
    load_tgt = pltpu.make_async_copy(tgt_hbm, tgt, load.at[1])
    load_src.start()
    load_tgt.start()

    col_peers = [(o, k) for o in range(NZ) for k in range(2) if (o, k) != (0, 0)]
    col_peers.sort(key=lambda p: -hops(p[0], NZ))
    y_peers = sorted(range(1, NY), key=lambda o: -hops(o, NY))
    x_peers = sorted(range(1, NX), key=lambda o: -hops(o, NX))

    def col_peer(o, k):
        return (row, ((z + o) % NZ) * 2 + (core + k) % 2)

    def y_peer(o):
        return (((y + o) % NY) * NX + x, col)

    def x_peer(o):
        return (y * NX + (x + o) % NX, col)

    col_ids = {p: col_peer(*p) for p in col_peers}
    y_ids = [y_peer(o) for o in y_peers]
    x_ids = [x_peer(o) for o in x_peers]
    peers = list(col_ids.values()) + y_ids + x_ids
    barrier = pltpu.get_barrier_semaphore()
    for peer in peers:
        pl.semaphore_signal(barrier, inc=1, device_id=peer, device_id_type=MESH)

    def copy(src_ref, dst_ref, send, recv, peer):
        return pltpu.make_async_remote_copy(
            src_ref=src_ref, dst_ref=dst_ref, send_sem=send, recv_sem=recv,
            device_id=peer, device_id_type=MESH,
        )

    load_src.wait()
    xs = normalize(src[...])
    nx_row = jnp.sum(xs * xs, axis=0, keepdims=True) * SCALE
    for b in range(nsb):
        nx[b : b + 1, :] = nx_row[:, b * LANES : (b + 1) * LANES]
    xs = xs * (2.0 * SCALE)
    first = lax.broadcasted_iota(jnp.int32, (LANES, LANES), 1) < d
    lane = lax.broadcasted_iota(jnp.int32, (LANES, LANES), 1)
    for b in range(nsb):
        blk = xs[:, b * LANES : (b + 1) * LANES]
        both = jnp.concatenate([blk, blk], axis=0).T
        x1 = both.astype(jnp.bfloat16).astype(jnp.float32)
        r = both - x1
        x2 = r.astype(jnp.bfloat16).astype(jnp.float32)
        rows = pl.ds(b * LANES, LANES)
        xk[rows, 0:128] = x1.astype(jnp.bfloat16)
        xk[rows, 128:256] = x2.astype(jnp.bfloat16)
        xk[rows, 256:384] = jnp.where(first, x1, r - x2).astype(jnp.bfloat16)
    load_tgt.wait()
    ys = normalize(tgt[...])
    tgt[...] = ys
    ny_row = jnp.sum(ys * ys, axis=0, keepdims=True) * SCALE
    for b in range(ntb):
        ny[b : b + 1, :] = ny_row[:, b * LANES : (b + 1) * LANES]
    y1, y2, y3 = split3(ys)
    for i, part in enumerate((y1, y2, y1, y2, y3, y1)):
        yk[i * d : (i + 1) * d, :] = part
    gpot[...] = -ny[...]

    def build_map_operand():
        for b in range(ntb):
            blk = tgt[:, b * LANES : (b + 1) * LANES]
            yt[b * LANES : (b + 1) * LANES, :] = jnp.concatenate(
                [blk, jnp.ones((LANES - d, LANES), jnp.float32)], axis=0
            ).T

    def score_tiles(c):
        rows = slice(c * 256, (c + 1) * 256)
        for n in range(nt // 256):
            lanes = slice(n * 256, (n + 1) * 256)

            def tile():
                score[rows, lanes] = jnp.dot(
                    xk[rows, :], yk[:, lanes], preferred_element_type=jnp.float32
                )

            yield tile

    def row_group(base, size):
        rows = pl.ds(base, size)
        ts = [score[rows, k * LANES : (k + 1) * LANES] + gpot[k : k + 1, :] for k in range(ntb)]
        top = tree(jnp.maximum, ts)
        part_m[rows, :] = top
        part_p[rows, :] = tree(jnp.add, [jnp.exp2(t - top) for t in ts])

    def plan_group(base, size, lo, hi):
        rows = pl.ds(base, size)
        pot = fcol[rows, :]
        ps = []
        for k in range(lo, hi):
            lanes = slice(k * LANES, (k + 1) * LANES)
            p = jnp.exp2((score[rows, lanes] + pot) + gpot[k : k + 1, :])
            plan[rows, lanes] = p
            ps.append(p)
        tot = tree(jnp.add, ps)
        part_p[rows, :] = tot if lo == 0 else tot + part_p[rows, :]

    def send_rows(step, c):
        for i in range(nsb // PARTS):
            b = c * (nsb // PARTS) + i
            pt = part_p[b * LANES : (b + 1) * LANES, :].T
            if step == 0:
                mt = part_m[b * LANES : (b + 1) * LANES, :].T
                top = jnp.max(mt, axis=0, keepdims=True)
                tot = jnp.sum(pt * jnp.exp2(mt - top), axis=0, keepdims=True)
                a_loc[step, c, i : i + 1, :] = top + jnp.log2(tot)
            else:
                a_loc[step, c, i : i + 1, :] = jnp.sum(pt, axis=0, keepdims=True)
        if step == 0 and c == 0:
            pl.semaphore_wait(barrier, len(peers))
        for o, k in col_peers:
            copy(
                a_loc.at[step, c], a_all.at[step, c, col],
                s_a.at[step], r_a.at[step, c], col_peer(o, k),
            ).start()

    def first_row_pass():
        count = ns // 256
        for c in range(count + 1):
            tiles = score_tiles(c) if c < count else [lambda: None] * (nt // 256)
            for n, tile in enumerate(tiles):
                tile()
                if c > 0:
                    for q in range(2):
                        row_group((c - 1) * 256 + n * 32 + q * 16, 16)
            if c > 0 and c % (count // PARTS) == 0:
                send_rows(0, c // (count // PARTS) - 1)

    def later_row_pass(step):
        wide = ntb // PARTS
        for c in range(PARTS):
            receive_b(step - 1, c)
            size = ns // PARTS
            for h in range(PARTS):

                def group(q, _):
                    base = pl.multiple_of(h * size + q * 32, 32)
                    plan_group(base, 32, c * wide, (c + 1) * wide)
                    return 0

                lax.fori_loop(0, size // 32, group, 0, unroll=8)
                if c == PARTS - 1:
                    send_rows(step, h)

    def receive_a(step, c):
        a_all[step, c, col] = a_loc[step, c]
        got = a_all.at[step, c, 0 : NC - 1]
        copy(got, got, s_a.at[step], r_a.at[step, c], peers[0]).wait_recv()
        size = nsb // PARTS
        part = slice(c * size, (c + 1) * size)
        if step == 0:
            pot = math.log2(n_tgt_total) - lse2([a_all[step, c, i] for i in range(NC)])
            fpot[part, :] = pot
        else:
            tot = tree(jnp.add, [a_all[step, c, i] for i in range(NC)])
            pot = (n_tgt_total / n_src_total) / tot
            f_out[part, :] = (fpot[part, :] + jnp.log2(pot) + nx[part, :]) * UNSCALE
        for i in range(size):
            b = c * size + i
            fcol[b * LANES : (b + 1) * LANES, :] = jnp.broadcast_to(
                pot[i : i + 1, :], (LANES, LANES)
            ).T

    def col_pass(step):
        wide = ntb // PARTS
        size = ns // PARTS
        for h in range(PARTS):
            receive_a(step, h)
            for c in range(PARTS):
                tops, accs = [None] * wide, [None] * wide
                if h > 0:
                    for k in range(wide):
                        lanes = slice((c * wide + k) * LANES, (c * wide + k + 1) * LANES)
                        tops[k], accs[k] = col_m[:, lanes], col_p[:, lanes]
                for b in range(size // 64):
                    for k in range(wide):
                        lanes = slice((c * wide + k) * LANES, (c * wide + k + 1) * LANES)
                        rows = slice(h * size + b * 64, h * size + (b + 1) * 64)
                        ts = (score[rows, lanes] + fcol[rows, :]).reshape(8, 8, LANES)
                        new = jnp.max(ts, axis=0)
                        if tops[k] is not None:
                            new = jnp.maximum(new, tops[k])
                        add = jnp.sum(jnp.exp2(ts - new[None]), axis=0)
                        if tops[k] is not None:
                            add += accs[k] * jnp.exp2(tops[k] - new)
                        tops[k], accs[k] = new, add
                for k in range(wide):
                    if h < PARTS - 1:
                        lanes = slice((c * wide + k) * LANES, (c * wide + k + 1) * LANES)
                        col_m[:, lanes], col_p[:, lanes] = tops[k], accs[k]
                    else:
                        full = jnp.max(tops[k], axis=0, keepdims=True)
                        tot = jnp.sum(accs[k] * jnp.exp2(tops[k] - full), axis=0, keepdims=True)
                        b_loc[step, c, k : k + 1, :] = full + jnp.log2(tot)
                if h == PARTS - 1:
                    send_cols(step, c)

    def plan_col_pass(step):
        wide = ntb // PARTS
        size = ns // PARTS
        for h in range(PARTS):
            receive_a(step, h)
            for c in range(PARTS):
                accs = [None] * wide
                for b in range(size // 64):
                    rows = slice(h * size + b * 64, h * size + (b + 1) * 64)
                    for k in range(wide):
                        lanes = slice((c * wide + k) * LANES, (c * wide + k + 1) * LANES)
                        ps = (plan[rows, lanes] * fcol[rows, :]).reshape(8, 8, LANES)
                        add = jnp.sum(ps, axis=0)
                        accs[k] = add if accs[k] is None else accs[k] + add
                for k in range(wide):
                    lanes = slice((c * wide + k) * LANES, (c * wide + k + 1) * LANES)
                    if h > 0:
                        accs[k] += col_p[:, lanes]
                    if h < PARTS - 1:
                        col_p[:, lanes] = accs[k]
                    else:
                        b_loc[step, c, k : k + 1, :] = jnp.sum(accs[k], axis=0, keepdims=True)
                if h == PARTS - 1:
                    send_cols(step, c)

    def send_cols(step, c):
        for peer in y_ids:
            copy(
                b_loc.at[step, c], b_y.at[step, c, y], s_by.at[step], r_by.at[step, c], peer
            ).start()

    def relay_cols(step, c):
        b_y[step, c, y] = b_loc[step, c]
        got = b_y.at[step, c, 0 : NY - 1]
        copy(got, got, s_by.at[step], r_by.at[step, c], peers[0]).wait_recv()
        parts = [b_y[step, c, i] for i in range(NY)]
        b_mid[step, c] = lse2(parts) if step == 0 else tree(jnp.add, parts)
        for peer in x_ids:
            copy(
                b_mid.at[step, c], b_x.at[step, c, x], s_bx.at[step], r_bx.at[step, c], peer
            ).start()

    def receive_b(step, c):
        b_x[step, c, x] = b_mid[step, c]
        got = b_x.at[step, c, 0 : NX - 1]
        copy(got, got, s_bx.at[step], r_bx.at[step, c], peers[0]).wait_recv()
        part = slice(c * (ntb // PARTS), (c + 1) * (ntb // PARTS))
        if step == 0:
            gpot[part, :] = -lse2([b_x[step, c, i] for i in range(NX)])
        else:
            fac = 1.0 / tree(jnp.add, [b_x[step, c, i] for i in range(NX)])
            g_out[part, :] = (
                gpot[part, :] + (jnp.log2(fac) + math.log2(n_src_total)) + ny[part, :]
            ) * UNSCALE
            for i in range(ntb // PARTS):
                b = c * (ntb // PARTS) + i
                rows = slice(b * LANES, (b + 1) * LANES)
                val = yt[rows, :] * jnp.broadcast_to(fac[i : i + 1, :], (LANES, LANES)).T
                v1 = val.astype(jnp.bfloat16)
                yv[rows, 0:LANES] = v1
                yv[rows, LANES : 2 * LANES] = (val - v1.astype(jnp.float32)).astype(jnp.bfloat16)

    order = sorted(range(NZ), key=lambda o: -hops(o, NZ))

    def split_plan():
        for t in range(NZ):
            base = pl.multiple_of((z + order[t]) % NZ * LANES, LANES)
            for q in range(LANES // 16):
                p = plan[pl.ds(pl.multiple_of(base + q * 16, 16), 16), :]
                p1 = p.astype(jnp.bfloat16)
                at = t * 2 * LANES + q * 16
                halves[at : at + 16, :] = p1
                halves[at + LANES : at + LANES + 16, :] = (
                    p - p1.astype(jnp.float32)
                ).astype(jnp.bfloat16)

    first_row_pass()
    build_map_operand()
    col_pass(0)
    for c in range(PARTS):
        relay_cols(0, c)
    later_row_pass(1)
    plan_col_pass(1)
    split_plan()
    for c in range(PARTS):
        relay_cols(1, c)

    half = d // 2
    partner = col_peer(0, 1)

    def product(t, count, c):
        part = slice(c * (nt // PARTS), (c + 1) * (nt // PARTS))
        rows = slice(t * 2 * LANES, (t + count) * 2 * LANES)
        both = jnp.dot(halves[rows, part], yv[part, :], preferred_element_type=jnp.float32)
        both = both[:, :LANES] + both[:, LANES:]
        out = []
        for i in range(count):
            at = i * 2 * LANES
            out.append(both[at : at + LANES] + both[at + LANES : at + 2 * LANES])
        return out

    for c in range(PARTS - 1):
        receive_b(1, c)
        for t, res in enumerate(product(0, NZ, c)):
            m_acc[t] = res if c == 0 else m_acc[t] + res
    receive_b(1, PARTS - 1)

    GROUP = 2

    def pair_copy(g):
        part = pl.ds(g * GROUP, GROUP)
        return copy(c_give.at[part], c_pair.at[part], s_p.at[0], r_p.at[g], partner)

    def finish_group(g):
        for i, res in enumerate(product(g * GROUP, GROUP, PARTS - 1)):
            t = g * GROUP + i
            res = (m_acc[t] + res).T
            c_mine[t, 0:half, :] = jnp.where(core == 0, res[:half], res[half:d])
            c_give[t, 0:half, :] = jnp.where(core == 0, res[half:d], res[:half])
            c_mine[t, half : half + 1, :] = res[d : d + 1]
            c_give[t, half : half + 1, :] = res[d : d + 1]
        pair_copy(g).start()

    def merge_group(g):
        pair_copy(g).wait_recv()
        for t in range(g * GROUP, (g + 1) * GROUP):
            if order[t] == 0:
                c_in[z] = c_mine[t] + c_pair[t]
            else:
                c_sum[t] = c_mine[t] + c_pair[t]
        for t in range(g * GROUP, (g + 1) * GROUP):
            if order[t] != 0:
                copy(c_sum.at[t], c_in.at[z], s_c.at[0], r_c.at[0], col_peer(order[t], 0)).start()

    for g in range(NZ // GROUP):
        finish_group(g)
        if g > 0:
            merge_group(g - 1)
    merge_group(NZ // GROUP - 1)
    got = c_in.at[0 : NZ - 1]
    c_whole = copy(got, got, s_c.at[0], r_c.at[0], peers[0])
    c_whole.wait_recv()
    tot = tree(jnp.add, [c_in[i] for i in range(NZ)])
    c_res[...] = tot[:half] / tot[half : half + 1]

    def gather_copy(o, k):
        return copy(c_res, c_all.at[core, z], s_g.at[0], r_g.at[o, k], col_peer(o, k))

    def relay_copy(o):
        piece = c_all.at[core, (z + NZ - o) % NZ]
        return copy(piece, piece, s_g.at[0], r_g.at[o, 1], partner)

    direct = NZ // 2
    for o in order[:-1]:
        gather_copy(o, 0).start()
        if o == direct:
            gather_copy(o, 1).start()
    gather_copy(0, 1).start()
    c_all[core, z] = c_res[...]
    for o in order[::-1][1:-1]:
        gather_copy(o, 0).wait_recv()
        relay_copy(o).start()

    for step in range(ITERS):
        a_got = a_all.at[step, :, 0 : NC - 1]
        y_got, x_got = b_y.at[step, :, 0 : NY - 1], b_x.at[step, :, 0 : NX - 1]
        copy(a_got, a_got, s_a.at[step], r_a.at[step, 0], peers[0]).wait_send()
        copy(y_got, y_got, s_by.at[step], r_by.at[step, 0], peers[0]).wait_send()
        copy(x_got, x_got, s_bx.at[step], r_bx.at[step, 0], peers[0]).wait_send()
    copy(c_give, c_give, s_p.at[0], r_p.at[0], partner).wait_send()
    c_whole.wait_send()
    gather_copy(direct, 0).wait_recv()
    for o in range(NZ):
        gather_copy(o, 1).wait_recv()
    for k in range(2):
        for i in range(NZ):
            m_out[k * half : (k + 1) * half, i * LANES : (i + 1) * LANES] = c_all[k, i]
    flat = c_all.at[0, 0 : NZ - 1]
    copy(c_all.at[0], c_all.at[0], s_g.at[0], r_g.at[0, 0], partner).wait_send()
    copy(flat, flat, s_g.at[0], r_g.at[0, 0], partner).wait_send()


def write_kernel(f, g, m, f_out, g_out, m_out, sems):
    copies = [
        pltpu.make_async_copy(a, b, sems.at[i])
        for i, (a, b) in enumerate(((m, m_out), (g, g_out), (f, f_out)))
    ]
    for c in copies:
        c.start()
    for c in copies:
        c.wait()


def solution(mesh):
    nrow, ncol = mesh.shape["row"], mesh.shape["col"]

    def shards(source, target):
        d, ns = source.shape
        nt = target.shape[1]
        nsb, ntb = ns // LANES, nt // LANES
        half = d // 2
        f32, bf16 = jnp.float32, jnp.bfloat16
        vmem = pltpu.VMEM
        dma = pltpu.SemaphoreType.DMA
        f, g, m = pl.pallas_call(
            functools.partial(kernel, ns * nrow, nt * ncol),
            out_shape=(
                jax.ShapeDtypeStruct((nsb, LANES), f32),
                jax.ShapeDtypeStruct((ntb, LANES), f32),
                jax.ShapeDtypeStruct((d, ns), f32),
            ),
            in_specs=[pl.BlockSpec(memory_space=pltpu.HBM)] * 2,
            out_specs=(pl.BlockSpec(memory_space=vmem),) * 3,
            scratch_shapes=[
                vmem((d, ns), f32),
                vmem((d, nt), f32),
                vmem((ns, 6 * d), bf16),
                vmem((6 * d, nt), bf16),
                vmem((nt, LANES), f32),
                vmem((nt, 2 * LANES), bf16),
                vmem((ns, nt), f32),
                vmem((ns, nt), f32),
                vmem((NZ * 2 * LANES, nt), bf16),
                vmem((NZ, LANES, LANES), f32),
                vmem((nsb, LANES), f32),
                vmem((ntb, LANES), f32),
                vmem((nsb, LANES), f32),
                vmem((ntb, LANES), f32),
                vmem((ns, LANES), f32),
                vmem((ns, LANES), f32),
                vmem((ns, LANES), f32),
                vmem((8, nt), f32),
                vmem((8, nt), f32),
                vmem((ITERS, PARTS, nsb // PARTS, LANES), f32),
                vmem((ITERS, PARTS, NC, nsb // PARTS, LANES), f32),
                vmem((ITERS, PARTS, ntb // PARTS, LANES), f32),
                vmem((ITERS, PARTS, NY, ntb // PARTS, LANES), f32),
                vmem((ITERS, PARTS, ntb // PARTS, LANES), f32),
                vmem((ITERS, PARTS, NX, ntb // PARTS, LANES), f32),
                vmem((NZ, half + 1, LANES), f32),
                vmem((NZ, half + 1, LANES), f32),
                vmem((NZ, half + 1, LANES), f32),
                vmem((NZ, half + 1, LANES), f32),
                vmem((NZ, half + 1, LANES), f32),
                vmem((half, LANES), f32),
                vmem((2, NZ, half, LANES), f32),
                dma((2,)),
                dma((ITERS,)),
                dma((ITERS, PARTS)),
                dma((ITERS,)),
                dma((ITERS, PARTS)),
                dma((ITERS,)),
                dma((ITERS, PARTS)),
                dma((1,)),
                dma((NZ,)),
                dma((1,)),
                dma((1,)),
                dma((1,)),
                dma((NZ, 2)),
            ],
            compiler_params=pltpu.CompilerParams(
                collective_id=0, has_side_effects=True, vmem_limit_bytes=VMEM_GRANT
            ),
            name="sinkhorn",
        )(source, target)
        f, g, m = pl.pallas_call(
            write_kernel,
            out_shape=(
                jax.ShapeDtypeStruct((nsb, LANES), f32),
                jax.ShapeDtypeStruct((ntb, LANES), f32),
                jax.ShapeDtypeStruct((d, ns), f32),
            ),
            in_specs=[pl.BlockSpec(memory_space=pl.ANY)] * 3,
            out_specs=(pl.BlockSpec(memory_space=pl.ANY),) * 3,
            scratch_shapes=[dma((3,))],
            compiler_params=pltpu.CompilerParams(vmem_limit_bytes=2**20),
            name="write_results",
        )(f, g, m)
        return f.reshape(ns), g.reshape(nt), m

    return jax.shard_map(
        shards,
        mesh=mesh,
        in_specs=(P(None, "row"), P(None, "col")),
        out_specs=(P("row"), P("col"), P(None, "row")),
        check_vma=False,
    )
```

```python
import functools
import math

import jax
import jax.numpy as jnp
from jax import lax
from jax.experimental import pallas as pl
from jax.experimental.pallas import tpu as pltpu
from jax.sharding import PartitionSpec as P

MESH = pl.DeviceIdType.MESH
ITERS = 2
EPSILON = 0.005
SCALE = 1.0 / (EPSILON * math.log(2.0))
UNSCALE = EPSILON * math.log(2.0)
LANES = 128
NZ, NX, NY = 8, 4, 8
NC = 2 * NZ
VMEM_GRANT = 56_150_000
ROW_PARTS, COL_PARTS = 4, 2
GROUP = 2


def normalize(points):
    total = jnp.sum(points * points, axis=0, keepdims=True)
    return points / jnp.sqrt(total + 1e-06)


def split3(a):
    a1 = a.astype(jnp.bfloat16)
    r = a - a1.astype(jnp.float32)
    a2 = r.astype(jnp.bfloat16)
    a3 = (r - a2.astype(jnp.float32)).astype(jnp.bfloat16)
    return a1, a2, a3


def tree(op, xs):
    xs = list(xs)
    while len(xs) > 1:
        xs = [op(xs[i], xs[i + 1]) if i + 1 < len(xs) else xs[i] for i in range(0, len(xs), 2)]
    return xs[0]


def lse2(xs):
    top = tree(jnp.maximum, xs)
    return top + jnp.log2(tree(jnp.add, [jnp.exp2(x - top) for x in xs]))


def hops(o, n):
    return min(o, n - o)


def kernel(
    n_src_total,
    n_tgt_total,
    src_hbm,
    tgt_hbm,
    f_out,
    g_out,
    m_out,
    src,
    tgt,
    xk,
    yk,
    yt,
    yv,
    score,
    plan,
    halves,
    m_acc,
    nx,
    ny,
    fpot,
    gpot,
    fcol,
    part_m,
    part_p,
    col_m,
    col_p,
    a_loc,
    a_all,
    b_loc,
    b_y,
    b_mid,
    b_x,
    c_mine,
    c_give,
    c_pair,
    c_sum,
    c_in,
    c_res,
    c_all,
    load,
    s_a,
    r_a,
    s_by,
    r_by,
    s_bx,
    r_bx,
    s_p,
    r_p,
    s_c,
    r_c,
    s_g,
    r_g,
):
    d, ns = src.shape
    nt = tgt.shape[1]
    nsb, ntb = ns // LANES, nt // LANES
    row, col = lax.axis_index("row"), lax.axis_index("col")
    y, x = row // NX, row % NX
    z, core = col // 2, col % 2

    load_src = pltpu.make_async_copy(src_hbm, src, load.at[0])
    load_tgt = pltpu.make_async_copy(tgt_hbm, tgt, load.at[1])
    load_src.start()
    load_tgt.start()

    col_peers = [(o, k) for o in range(NZ) for k in range(2) if (o, k) != (0, 0)]
    col_peers.sort(key=lambda p: -hops(p[0], NZ))
    y_peers = sorted(range(1, NY), key=lambda o: -hops(o, NY))
    x_peers = sorted(range(1, NX), key=lambda o: -hops(o, NX))

    def col_peer(o, k):
        return (row, ((z + o) % NZ) * 2 + (core + k) % 2)

    def y_peer(o):
        return (((y + o) % NY) * NX + x, col)

    def x_peer(o):
        return (y * NX + (x + o) % NX, col)

    col_ids = {p: col_peer(*p) for p in col_peers}
    y_ids = [y_peer(o) for o in y_peers]
    x_ids = [x_peer(o) for o in x_peers]
    peers = list(col_ids.values()) + y_ids + x_ids
    barrier = pltpu.get_barrier_semaphore()
    for peer in peers:
        pl.semaphore_signal(barrier, inc=1, device_id=peer, device_id_type=MESH)

    def copy(src_ref, dst_ref, send, recv, peer):
        return pltpu.make_async_remote_copy(
            src_ref=src_ref, dst_ref=dst_ref, send_sem=send, recv_sem=recv,
            device_id=peer, device_id_type=MESH,
        )

    load_src.wait()
    xs = normalize(src[...])
    nx_row = jnp.sum(xs * xs, axis=0, keepdims=True) * SCALE
    for b in range(nsb):
        nx[b : b + 1, :] = nx_row[:, b * LANES : (b + 1) * LANES]
    xs = xs * (2.0 * SCALE)
    first = lax.broadcasted_iota(jnp.int32, (LANES, LANES), 1) < d
    lane = lax.broadcasted_iota(jnp.int32, (LANES, LANES), 1)
    for b in range(nsb):
        blk = xs[:, b * LANES : (b + 1) * LANES]
        both = jnp.concatenate([blk, blk], axis=0).T
        x1 = both.astype(jnp.bfloat16).astype(jnp.float32)
        r = both - x1
        x2 = r.astype(jnp.bfloat16).astype(jnp.float32)
        rows = pl.ds(b * LANES, LANES)
        xk[rows, 0:128] = x1.astype(jnp.bfloat16)
        xk[rows, 128:256] = x2.astype(jnp.bfloat16)
        xk[rows, 256:384] = jnp.where(first, x1, r - x2).astype(jnp.bfloat16)
    load_tgt.wait()
    ys = normalize(tgt[...])
    tgt[...] = ys
    ny_row = jnp.sum(ys * ys, axis=0, keepdims=True) * SCALE
    for b in range(ntb):
        ny[b : b + 1, :] = ny_row[:, b * LANES : (b + 1) * LANES]
    y1, y2, y3 = split3(ys)
    for i, part in enumerate((y1, y2, y1, y2, y3, y1)):
        yk[i * d : (i + 1) * d, :] = part
    gpot[...] = -ny[...]

    def build_map_operand():
        for b in range(ntb):
            blk = tgt[:, b * LANES : (b + 1) * LANES]
            yt[b * LANES : (b + 1) * LANES, :] = jnp.concatenate(
                [blk, jnp.ones((LANES - d, LANES), jnp.float32)], axis=0
            ).T

    def score_tiles(c):
        rows = slice(c * 256, (c + 1) * 256)
        for n in range(nt // 256):
            lanes = slice(n * 256, (n + 1) * 256)

            def tile():
                score[rows, lanes] = jnp.dot(
                    xk[rows, :], yk[:, lanes], preferred_element_type=jnp.float32
                )

            yield tile

    def row_group(base, size):
        rows = pl.ds(base, size)
        ts = [score[rows, k * LANES : (k + 1) * LANES] + gpot[k : k + 1, :] for k in range(ntb)]
        top = tree(jnp.maximum, ts)
        part_m[rows, :] = top
        part_p[rows, :] = tree(jnp.add, [jnp.exp2(t - top) for t in ts])

    def plan_group(base, size, lo, hi):
        rows = pl.ds(base, size)
        pot = fcol[rows, :]
        ps = []
        for k in range(lo, hi):
            lanes = slice(k * LANES, (k + 1) * LANES)
            p = jnp.exp2((score[rows, lanes] + pot) + gpot[k : k + 1, :])
            plan[rows, lanes] = p
            ps.append(p)
        tot = tree(jnp.add, ps)
        part_p[rows, :] = tot if lo == 0 else tot + part_p[rows, :]

    def send_rows(step, c):
        for i in range(nsb // ROW_PARTS):
            b = c * (nsb // ROW_PARTS) + i
            pt = part_p[b * LANES : (b + 1) * LANES, :].T
            if step == 0:
                mt = part_m[b * LANES : (b + 1) * LANES, :].T
                top = jnp.max(mt, axis=0, keepdims=True)
                tot = jnp.sum(pt * jnp.exp2(mt - top), axis=0, keepdims=True)
                a_loc[step, c, i : i + 1, :] = top + jnp.log2(tot)
            else:
                a_loc[step, c, i : i + 1, :] = jnp.sum(pt, axis=0, keepdims=True)
        if step == 0 and c == 0:
            pl.semaphore_wait(barrier, len(peers))
        for o, k in col_peers:
            copy(
                a_loc.at[step, c], a_all.at[step, c, col],
                s_a.at[step], r_a.at[step, c], col_peer(o, k),
            ).start()

    def first_row_pass():
        count = ns // 256
        for c in range(count + 1):
            tiles = score_tiles(c) if c < count else [lambda: None] * (nt // 256)
            for n, tile in enumerate(tiles):
                tile()
                if c > 0:
                    for q in range(2):
                        row_group((c - 1) * 256 + n * 32 + q * 16, 16)
            if c > 0 and c % (count // ROW_PARTS) == 0:
                send_rows(0, c // (count // ROW_PARTS) - 1)

    def later_row_pass(step):
        wide = ntb // COL_PARTS
        tall = 256 // wide
        for c in range(COL_PARTS):
            receive_b(step - 1, c)
            size = ns // ROW_PARTS
            for h in range(ROW_PARTS):

                def group(q, _):
                    base = pl.multiple_of(h * size + q * tall, tall)
                    plan_group(base, tall, c * wide, (c + 1) * wide)
                    return 0

                lax.fori_loop(0, size // tall, group, 0, unroll=8)
                if c == COL_PARTS - 1:
                    send_rows(step, h)

    def receive_a(step, c):
        a_all[step, c, col] = a_loc[step, c]
        got = a_all.at[step, c, 0 : NC - 1]
        copy(got, got, s_a.at[step], r_a.at[step, c], peers[0]).wait_recv()
        size = nsb // ROW_PARTS
        part = slice(c * size, (c + 1) * size)
        if step == 0:
            pot = math.log2(n_tgt_total) - lse2([a_all[step, c, i] for i in range(NC)])
            fpot[part, :] = pot
        else:
            tot = tree(jnp.add, [a_all[step, c, i] for i in range(NC)])
            pot = (n_tgt_total / n_src_total) / tot
            f_out[part, :] = (fpot[part, :] + jnp.log2(pot) + nx[part, :]) * UNSCALE
        for i in range(size):
            b = c * size + i
            fcol[b * LANES : (b + 1) * LANES, :] = jnp.broadcast_to(
                pot[i : i + 1, :], (LANES, LANES)
            ).T

    def col_pass(step):
        wide = 8
        per = ntb // COL_PARTS // wide
        size = ns // ROW_PARTS
        for h in range(ROW_PARTS):
            receive_a(step, h)
            for c in range(ntb // wide):
                tops, accs = [None] * wide, [None] * wide
                if h > 0:
                    for k in range(wide):
                        lanes = slice((c * wide + k) * LANES, (c * wide + k + 1) * LANES)
                        tops[k], accs[k] = col_m[:, lanes], col_p[:, lanes]
                for b in range(size // 64):
                    for k in range(wide):
                        lanes = slice((c * wide + k) * LANES, (c * wide + k + 1) * LANES)
                        rows = slice(h * size + b * 64, h * size + (b + 1) * 64)
                        ts = (score[rows, lanes] + fcol[rows, :]).reshape(8, 8, LANES)
                        new = jnp.max(ts, axis=0)
                        if tops[k] is not None:
                            new = jnp.maximum(new, tops[k])
                        add = jnp.sum(jnp.exp2(ts - new[None]), axis=0)
                        if tops[k] is not None:
                            add += accs[k] * jnp.exp2(tops[k] - new)
                        tops[k], accs[k] = new, add
                for k in range(wide):
                    if h < ROW_PARTS - 1:
                        lanes = slice((c * wide + k) * LANES, (c * wide + k + 1) * LANES)
                        col_m[:, lanes], col_p[:, lanes] = tops[k], accs[k]
                    else:
                        full = jnp.max(tops[k], axis=0, keepdims=True)
                        tot = jnp.sum(accs[k] * jnp.exp2(tops[k] - full), axis=0, keepdims=True)
                        b_loc[step, c // per, c % per * wide + k : c % per * wide + k + 1, :] = full + jnp.log2(tot)
                if h == ROW_PARTS - 1 and c % per == per - 1:
                    send_cols(step, c // per)

    def plan_col_pass(step):
        wide = 8
        per = ntb // COL_PARTS // wide
        size = ns // ROW_PARTS
        for h in range(ROW_PARTS):
            receive_a(step, h)
            for c in range(ntb // wide):
                accs = [None] * wide
                for b in range(size // 64):
                    rows = slice(h * size + b * 64, h * size + (b + 1) * 64)
                    for k in range(wide):
                        lanes = slice((c * wide + k) * LANES, (c * wide + k + 1) * LANES)
                        ps = (plan[rows, lanes] * fcol[rows, :]).reshape(8, 8, LANES)
                        add = jnp.sum(ps, axis=0)
                        accs[k] = add if accs[k] is None else accs[k] + add
                for k in range(wide):
                    lanes = slice((c * wide + k) * LANES, (c * wide + k + 1) * LANES)
                    if h > 0:
                        accs[k] += col_p[:, lanes]
                    if h < ROW_PARTS - 1:
                        col_p[:, lanes] = accs[k]
                    else:
                        b_loc[step, c // per, c % per * wide + k : c % per * wide + k + 1, :] = jnp.sum(accs[k], axis=0, keepdims=True)
                if h == ROW_PARTS - 1 and c % per == per - 1:
                    send_cols(step, c // per)

    def send_cols(step, c):
        for peer in y_ids:
            copy(
                b_loc.at[step, c], b_y.at[step, c, y], s_by.at[step], r_by.at[step, c], peer
            ).start()

    def relay_cols(step, c):
        b_y[step, c, y] = b_loc[step, c]
        got = b_y.at[step, c, 0 : NY - 1]
        copy(got, got, s_by.at[step], r_by.at[step, c], peers[0]).wait_recv()
        parts = [b_y[step, c, i] for i in range(NY)]
        b_mid[step, c] = lse2(parts) if step == 0 else tree(jnp.add, parts)
        for peer in x_ids:
            copy(
                b_mid.at[step, c], b_x.at[step, c, x], s_bx.at[step], r_bx.at[step, c], peer
            ).start()

    def receive_b(step, c):
        b_x[step, c, x] = b_mid[step, c]
        got = b_x.at[step, c, 0 : NX - 1]
        copy(got, got, s_bx.at[step], r_bx.at[step, c], peers[0]).wait_recv()
        part = slice(c * (ntb // COL_PARTS), (c + 1) * (ntb // COL_PARTS))
        if step == 0:
            gpot[part, :] = -lse2([b_x[step, c, i] for i in range(NX)])
        else:
            fac = 1.0 / tree(jnp.add, [b_x[step, c, i] for i in range(NX)])
            g_out[part, :] = (
                gpot[part, :] + (jnp.log2(fac) + math.log2(n_src_total)) + ny[part, :]
            ) * UNSCALE
            for i in range(ntb // COL_PARTS):
                b = c * (ntb // COL_PARTS) + i
                rows = slice(b * LANES, (b + 1) * LANES)
                val = yt[rows, :] * jnp.broadcast_to(fac[i : i + 1, :], (LANES, LANES)).T
                v1 = val.astype(jnp.bfloat16)
                yv[rows, 0:LANES] = v1
                yv[rows, LANES : 2 * LANES] = (val - v1.astype(jnp.float32)).astype(jnp.bfloat16)

    order = sorted(range(NZ), key=lambda o: -hops(o, NZ))

    def split_plan():
        for t in range(NZ):
            base = pl.multiple_of((z + order[t]) % NZ * LANES, LANES)
            for q in range(LANES // 16):
                p = plan[pl.ds(pl.multiple_of(base + q * 16, 16), 16), :]
                p1 = p.astype(jnp.bfloat16)
                at = t * 2 * LANES + q * 16
                halves[at : at + 16, :] = p1
                halves[at + LANES : at + LANES + 16, :] = (
                    p - p1.astype(jnp.float32)
                ).astype(jnp.bfloat16)

    first_row_pass()
    build_map_operand()
    col_pass(0)
    for c in range(COL_PARTS):
        relay_cols(0, c)
    later_row_pass(1)
    plan_col_pass(1)
    split_plan()
    for c in range(COL_PARTS):
        relay_cols(1, c)

    half = d // 2
    partner = col_peer(0, 1)

    def product(t, count, c):
        part = slice(c * (nt // COL_PARTS), (c + 1) * (nt // COL_PARTS))
        rows = slice(t * 2 * LANES, (t + count) * 2 * LANES)
        both = jnp.dot(halves[rows, part], yv[part, :], preferred_element_type=jnp.float32)
        both = both[:, :LANES] + both[:, LANES:]
        out = []
        for i in range(count):
            at = i * 2 * LANES
            out.append(both[at : at + LANES] + both[at + LANES : at + 2 * LANES])
        return out

    for c in range(COL_PARTS - 1):
        receive_b(1, c)
        for t, res in enumerate(product(0, NZ, c)):
            m_acc[t] = res if c == 0 else m_acc[t] + res
    receive_b(1, COL_PARTS - 1)


    def pair_copy(g):
        part = pl.ds(g * GROUP, GROUP)
        return copy(c_give.at[part], c_pair.at[part], s_p.at[0], r_p.at[g], partner)

    def finish_group(g):
        for i, res in enumerate(product(g * GROUP, GROUP, COL_PARTS - 1)):
            t = g * GROUP + i
            res = (res if COL_PARTS == 1 else m_acc[t] + res).T
            c_mine[t, 0:half, :] = jnp.where(core == 0, res[:half], res[half:d])
            c_give[t, 0:half, :] = jnp.where(core == 0, res[half:d], res[:half])
            c_mine[t, half : half + 1, :] = res[d : d + 1]
            c_give[t, half : half + 1, :] = res[d : d + 1]
        pair_copy(g).start()

    def merge_group(g):
        pair_copy(g).wait_recv()
        for t in range(g * GROUP, (g + 1) * GROUP):
            if order[t] == 0:
                c_in[z] = c_mine[t] + c_pair[t]
            else:
                c_sum[t] = c_mine[t] + c_pair[t]
        for t in range(g * GROUP, (g + 1) * GROUP):
            if order[t] != 0:
                copy(c_sum.at[t], c_in.at[z], s_c.at[0], r_c.at[0], col_peer(order[t], 0)).start()

    for g in range(NZ // GROUP):
        finish_group(g)
        if g > 0:
            merge_group(g - 1)
    merge_group(NZ // GROUP - 1)
    got = c_in.at[0 : NZ - 1]
    c_whole = copy(got, got, s_c.at[0], r_c.at[0], peers[0])
    c_whole.wait_recv()
    tot = tree(jnp.add, [c_in[i] for i in range(NZ)])
    c_res[...] = tot[:half] / tot[half : half + 1]

    def gather_copy(o, k):
        return copy(c_res, c_all.at[core, z], s_g.at[0], r_g.at[o, k], col_peer(o, k))

    def relay_copy(o):
        piece = c_all.at[core, (z + NZ - o) % NZ]
        return copy(piece, piece, s_g.at[0], r_g.at[o, 1], partner)

    direct = NZ // 2
    for o in order[:-1]:
        gather_copy(o, 0).start()
        if o == direct:
            gather_copy(o, 1).start()
    gather_copy(0, 1).start()
    c_all[core, z] = c_res[...]
    for o in order[::-1][1:-1]:
        gather_copy(o, 0).wait_recv()
        relay_copy(o).start()

    for step in range(ITERS):
        a_got = a_all.at[step, :, 0 : NC - 1]
        y_got, x_got = b_y.at[step, :, 0 : NY - 1], b_x.at[step, :, 0 : NX - 1]
        copy(a_got, a_got, s_a.at[step], r_a.at[step, 0], peers[0]).wait_send()
        copy(y_got, y_got, s_by.at[step], r_by.at[step, 0], peers[0]).wait_send()
        copy(x_got, x_got, s_bx.at[step], r_bx.at[step, 0], peers[0]).wait_send()
    copy(c_give, c_give, s_p.at[0], r_p.at[0], partner).wait_send()
    c_whole.wait_send()
    gather_copy(direct, 0).wait_recv()
    for o in range(NZ):
        gather_copy(o, 1).wait_recv()
    for k in range(2):
        for i in range(NZ):
            m_out[k * half : (k + 1) * half, i * LANES : (i + 1) * LANES] = c_all[k, i]
    flat = c_all.at[0, 0 : NZ - 1]
    copy(c_all.at[0], c_all.at[0], s_g.at[0], r_g.at[0, 0], partner).wait_send()
    copy(flat, flat, s_g.at[0], r_g.at[0, 0], partner).wait_send()


def write_kernel(f, g, m, f_out, g_out, m_out, sems):
    copies = [
        pltpu.make_async_copy(a, b, sems.at[i])
        for i, (a, b) in enumerate(((m, m_out), (g, g_out), (f, f_out)))
    ]
    for c in copies:
        c.start()
    for c in copies:
        c.wait()


def solution(mesh):
    nrow, ncol = mesh.shape["row"], mesh.shape["col"]

    def shards(source, target):
        d, ns = source.shape
        nt = target.shape[1]
        nsb, ntb = ns // LANES, nt // LANES
        half = d // 2
        f32, bf16 = jnp.float32, jnp.bfloat16
        vmem = pltpu.VMEM
        dma = pltpu.SemaphoreType.DMA
        f, g, m = pl.pallas_call(
            functools.partial(kernel, ns * nrow, nt * ncol),
            out_shape=(
                jax.ShapeDtypeStruct((nsb, LANES), f32),
                jax.ShapeDtypeStruct((ntb, LANES), f32),
                jax.ShapeDtypeStruct((d, ns), f32),
            ),
            in_specs=[pl.BlockSpec(memory_space=pltpu.HBM)] * 2,
            out_specs=(pl.BlockSpec(memory_space=vmem),) * 3,
            scratch_shapes=[
                vmem((d, ns), f32),
                vmem((d, nt), f32),
                vmem((ns, 6 * d), bf16),
                vmem((6 * d, nt), bf16),
                vmem((nt, LANES), f32),
                vmem((nt, 2 * LANES), bf16),
                vmem((ns, nt), f32),
                vmem((ns, nt), f32),
                vmem((NZ * 2 * LANES, nt), bf16),
                vmem((NZ, LANES, LANES), f32),
                vmem((nsb, LANES), f32),
                vmem((ntb, LANES), f32),
                vmem((nsb, LANES), f32),
                vmem((ntb, LANES), f32),
                vmem((ns, LANES), f32),
                vmem((ns, LANES), f32),
                vmem((ns, LANES), f32),
                vmem((8, nt), f32),
                vmem((8, nt), f32),
                vmem((ITERS, ROW_PARTS, nsb // ROW_PARTS, LANES), f32),
                vmem((ITERS, ROW_PARTS, NC, nsb // ROW_PARTS, LANES), f32),
                vmem((ITERS, COL_PARTS, ntb // COL_PARTS, LANES), f32),
                vmem((ITERS, COL_PARTS, NY, ntb // COL_PARTS, LANES), f32),
                vmem((ITERS, COL_PARTS, ntb // COL_PARTS, LANES), f32),
                vmem((ITERS, COL_PARTS, NX, ntb // COL_PARTS, LANES), f32),
                vmem((NZ, half + 1, LANES), f32),
                vmem((NZ, half + 1, LANES), f32),
                vmem((NZ, half + 1, LANES), f32),
                vmem((NZ, half + 1, LANES), f32),
                vmem((NZ, half + 1, LANES), f32),
                vmem((half, LANES), f32),
                vmem((2, NZ, half, LANES), f32),
                dma((2,)),
                dma((ITERS,)),
                dma((ITERS, ROW_PARTS)),
                dma((ITERS,)),
                dma((ITERS, COL_PARTS)),
                dma((ITERS,)),
                dma((ITERS, COL_PARTS)),
                dma((1,)),
                dma((NZ,)),
                dma((1,)),
                dma((1,)),
                dma((1,)),
                dma((NZ, 2)),
            ],
            compiler_params=pltpu.CompilerParams(
                collective_id=0, has_side_effects=True, vmem_limit_bytes=VMEM_GRANT
            ),
            name="sinkhorn",
        )(source, target)
        f, g, m = pl.pallas_call(
            write_kernel,
            out_shape=(
                jax.ShapeDtypeStruct((nsb, LANES), f32),
                jax.ShapeDtypeStruct((ntb, LANES), f32),
                jax.ShapeDtypeStruct((d, ns), f32),
            ),
            in_specs=[pl.BlockSpec(memory_space=pl.ANY)] * 3,
            out_specs=(pl.BlockSpec(memory_space=pl.ANY),) * 3,
            scratch_shapes=[dma((3,))],
            compiler_params=pltpu.CompilerParams(vmem_limit_bytes=2**20),
            name="write_results",
        )(f, g, m)
        return f.reshape(ns), g.reshape(nt), m

    return jax.shard_map(
        shards,
        mesh=mesh,
        in_specs=(P(None, "row"), P(None, "col")),
        out_specs=(P("row"), P("col"), P(None, "row")),
        check_vma=False,
    )
```

```python
import functools
import math

import jax
import jax.numpy as jnp
from jax import lax
from jax.experimental import pallas as pl
from jax.experimental.pallas import tpu as pltpu
from jax.sharding import PartitionSpec as P

MESH = pl.DeviceIdType.MESH
ITERS = 2
EPSILON = 0.005
SCALE = 1.0 / (EPSILON * math.log(2.0))
UNSCALE = EPSILON * math.log(2.0)
LANES = 128
NZ, NX, NY = 8, 4, 8
NC = 2 * NZ
VMEM_GRANT = 56_150_000
ROW_PARTS, COL_PARTS = 2, 2
GROUP = 2


def normalize(points):
    total = jnp.sum(points * points, axis=0, keepdims=True)
    return points / jnp.sqrt(total + 1e-06)


def split3(a):
    a1 = a.astype(jnp.bfloat16)
    r = a - a1.astype(jnp.float32)
    a2 = r.astype(jnp.bfloat16)
    a3 = (r - a2.astype(jnp.float32)).astype(jnp.bfloat16)
    return a1, a2, a3


def tree(op, xs):
    xs = list(xs)
    while len(xs) > 1:
        xs = [op(xs[i], xs[i + 1]) if i + 1 < len(xs) else xs[i] for i in range(0, len(xs), 2)]
    return xs[0]


def lse2(xs):
    top = tree(jnp.maximum, xs)
    return top + jnp.log2(tree(jnp.add, [jnp.exp2(x - top) for x in xs]))


def hops(o, n):
    return min(o, n - o)


def kernel(
    n_src_total,
    n_tgt_total,
    src_hbm,
    tgt_hbm,
    f_out,
    g_out,
    m_out,
    src,
    tgt,
    xk,
    yk,
    yt,
    yv,
    score,
    plan,
    halves,
    m_acc,
    nx,
    ny,
    fpot,
    gpot,
    fcol,
    part_m,
    part_p,
    col_m,
    col_p,
    a_loc,
    a_all,
    b_loc,
    b_y,
    b_mid,
    b_x,
    c_mine,
    c_give,
    c_pair,
    c_out,
    c_in,
    c_res,
    c_all,
    load,
    s_a,
    r_a,
    s_by,
    r_by,
    s_bx,
    r_bx,
    s_p,
    r_p,
    s_c,
    r_c,
    s_g,
    r_g,
):
    d, ns = src.shape
    nt = tgt.shape[1]
    nsb, ntb = ns // LANES, nt // LANES
    row, col = lax.axis_index("row"), lax.axis_index("col")
    y, x = row // NX, row % NX
    z, core = col // 2, col % 2

    load_src = pltpu.make_async_copy(src_hbm, src, load.at[0])
    load_tgt = pltpu.make_async_copy(tgt_hbm, tgt, load.at[1])
    load_src.start()
    load_tgt.start()

    col_peers = [(o, k) for o in range(NZ) for k in range(2) if (o, k) != (0, 0)]
    col_peers.sort(key=lambda p: -hops(p[0], NZ))
    y_peers = sorted(range(1, NY), key=lambda o: -hops(o, NY))
    x_peers = sorted(range(1, NX), key=lambda o: -hops(o, NX))

    def col_peer(o, k):
        return (row, ((z + o) % NZ) * 2 + (core + k) % 2)

    def y_peer(o):
        return (((y + o) % NY) * NX + x, col)

    def x_peer(o):
        return (y * NX + (x + o) % NX, col)

    col_ids = {p: col_peer(*p) for p in col_peers}
    y_ids = [y_peer(o) for o in y_peers]
    x_ids = [x_peer(o) for o in x_peers]
    peers = list(col_ids.values()) + y_ids + x_ids
    barrier = pltpu.get_barrier_semaphore()
    for peer in peers:
        pl.semaphore_signal(barrier, inc=1, device_id=peer, device_id_type=MESH)

    def copy(src_ref, dst_ref, send, recv, peer):
        return pltpu.make_async_remote_copy(
            src_ref=src_ref, dst_ref=dst_ref, send_sem=send, recv_sem=recv,
            device_id=peer, device_id_type=MESH,
        )

    load_src.wait()
    xs = normalize(src[...])
    nx_row = jnp.sum(xs * xs, axis=0, keepdims=True) * SCALE
    for b in range(nsb):
        nx[b : b + 1, :] = nx_row[:, b * LANES : (b + 1) * LANES]
    xs = xs * (2.0 * SCALE)
    first = lax.broadcasted_iota(jnp.int32, (LANES, LANES), 1) < d
    lane = lax.broadcasted_iota(jnp.int32, (LANES, LANES), 1)
    for b in range(nsb):
        blk = xs[:, b * LANES : (b + 1) * LANES]
        both = jnp.concatenate([blk, blk], axis=0).T
        x1 = both.astype(jnp.bfloat16).astype(jnp.float32)
        r = both - x1
        x2 = r.astype(jnp.bfloat16).astype(jnp.float32)
        rows = pl.ds(b * LANES, LANES)
        xk[rows, 0:128] = x1.astype(jnp.bfloat16)
        xk[rows, 128:256] = x2.astype(jnp.bfloat16)
        xk[rows, 256:384] = jnp.where(first, x1, r - x2).astype(jnp.bfloat16)
    load_tgt.wait()
    ys = normalize(tgt[...])
    tgt[...] = ys
    ny_row = jnp.sum(ys * ys, axis=0, keepdims=True) * SCALE
    for b in range(ntb):
        ny[b : b + 1, :] = ny_row[:, b * LANES : (b + 1) * LANES]
    y1, y2, y3 = split3(ys)
    for i, part in enumerate((y1, y2, y1, y2, y3, y1)):
        yk[i * d : (i + 1) * d, :] = part
    gpot[...] = -ny[...]

    def build_map_operand():
        for b in range(ntb):
            blk = tgt[:, b * LANES : (b + 1) * LANES]
            yt[b * LANES : (b + 1) * LANES, :] = jnp.concatenate(
                [blk, jnp.ones((LANES - d, LANES), jnp.float32)], axis=0
            ).T

    def score_tiles(c):
        rows = slice(c * 256, (c + 1) * 256)
        for n in range(nt // 256):
            lanes = slice(n * 256, (n + 1) * 256)

            def tile():
                score[rows, lanes] = jnp.dot(
                    xk[rows, :], yk[:, lanes], preferred_element_type=jnp.float32
                )

            yield tile

    def row_group(base, size):
        rows = pl.ds(base, size)
        ts = [score[rows, k * LANES : (k + 1) * LANES] + gpot[k : k + 1, :] for k in range(ntb)]
        top = tree(jnp.maximum, ts)
        part_m[rows, :] = top
        part_p[rows, :] = tree(jnp.add, [jnp.exp2(t - top) for t in ts])

    def plan_group(base, size, lo, hi):
        rows = pl.ds(base, size)
        pot = fcol[rows, :]
        ps = []
        for k in range(lo, hi):
            lanes = slice(k * LANES, (k + 1) * LANES)
            p = jnp.exp2((score[rows, lanes] + pot) + gpot[k : k + 1, :])
            plan[rows, lanes] = p
            ps.append(p)
        tot = tree(jnp.add, ps)
        part_p[rows, :] = tot if lo == 0 else tot + part_p[rows, :]

    def send_rows(step, c):
        for i in range(nsb // ROW_PARTS):
            b = c * (nsb // ROW_PARTS) + i
            pt = part_p[b * LANES : (b + 1) * LANES, :].T
            if step == 0:
                mt = part_m[b * LANES : (b + 1) * LANES, :].T
                top = jnp.max(mt, axis=0, keepdims=True)
                tot = jnp.sum(pt * jnp.exp2(mt - top), axis=0, keepdims=True)
                a_loc[step, c, i : i + 1, :] = top + jnp.log2(tot)
            else:
                a_loc[step, c, i : i + 1, :] = jnp.sum(pt, axis=0, keepdims=True)
        if step == 0 and c == 0:
            pl.semaphore_wait(barrier, len(peers))
        for o, k in col_peers:
            copy(
                a_loc.at[step, c], a_all.at[step, c, col],
                s_a.at[step], r_a.at[step, c], col_peer(o, k),
            ).start()

    def first_row_pass():
        count = ns // 256
        for c in range(count + 1):
            tiles = score_tiles(c) if c < count else [lambda: None] * (nt // 256)
            for n, tile in enumerate(tiles):
                tile()
                if c > 0:
                    for q in range(2):
                        row_group((c - 1) * 256 + n * 32 + q * 16, 16)
            if c > 0 and c % (count // ROW_PARTS) == 0:
                send_rows(0, c // (count // ROW_PARTS) - 1)

    def later_row_pass(step):
        wide = ntb // COL_PARTS
        tall = 256 // wide
        for c in range(COL_PARTS):
            receive_b(step - 1, c)
            size = ns // ROW_PARTS
            for h in range(ROW_PARTS):

                def group(q, _):
                    base = pl.multiple_of(h * size + q * tall, tall)
                    plan_group(base, tall, c * wide, (c + 1) * wide)
                    return 0

                lax.fori_loop(0, size // tall, group, 0, unroll=8)
                if c == COL_PARTS - 1:
                    send_rows(step, h)

    def receive_a(step, c):
        a_all[step, c, col] = a_loc[step, c]
        got = a_all.at[step, c, 0 : NC - 1]
        copy(got, got, s_a.at[step], r_a.at[step, c], peers[0]).wait_recv()
        size = nsb // ROW_PARTS
        part = slice(c * size, (c + 1) * size)
        if step == 0:
            pot = math.log2(n_tgt_total) - lse2([a_all[step, c, i] for i in range(NC)])
            fpot[part, :] = pot
        else:
            tot = tree(jnp.add, [a_all[step, c, i] for i in range(NC)])
            pot = (n_tgt_total / n_src_total) / tot
            f_out[part, :] = (fpot[part, :] + jnp.log2(pot) + nx[part, :]) * UNSCALE
        for i in range(size):
            b = c * size + i
            fcol[b * LANES : (b + 1) * LANES, :] = jnp.broadcast_to(
                pot[i : i + 1, :], (LANES, LANES)
            ).T

    def col_pass(step):
        wide = 8
        per = ntb // COL_PARTS // wide
        size = ns // ROW_PARTS
        for h in range(ROW_PARTS):
            receive_a(step, h)
            for c in range(ntb // wide):
                tops, accs = [None] * wide, [None] * wide
                if h > 0:
                    for k in range(wide):
                        lanes = slice((c * wide + k) * LANES, (c * wide + k + 1) * LANES)
                        tops[k], accs[k] = col_m[:, lanes], col_p[:, lanes]
                for b in range(size // 64):
                    for k in range(wide):
                        lanes = slice((c * wide + k) * LANES, (c * wide + k + 1) * LANES)
                        rows = slice(h * size + b * 64, h * size + (b + 1) * 64)
                        ts = (score[rows, lanes] + fcol[rows, :]).reshape(8, 8, LANES)
                        new = jnp.max(ts, axis=0)
                        if tops[k] is not None:
                            new = jnp.maximum(new, tops[k])
                        add = jnp.sum(jnp.exp2(ts - new[None]), axis=0)
                        if tops[k] is not None:
                            add += accs[k] * jnp.exp2(tops[k] - new)
                        tops[k], accs[k] = new, add
                for k in range(wide):
                    if h < ROW_PARTS - 1:
                        lanes = slice((c * wide + k) * LANES, (c * wide + k + 1) * LANES)
                        col_m[:, lanes], col_p[:, lanes] = tops[k], accs[k]
                    else:
                        full = jnp.max(tops[k], axis=0, keepdims=True)
                        tot = jnp.sum(accs[k] * jnp.exp2(tops[k] - full), axis=0, keepdims=True)
                        b_loc[step, c // per, c % per * wide + k : c % per * wide + k + 1, :] = full + jnp.log2(tot)
                if h == ROW_PARTS - 1 and c % per == per - 1:
                    send_cols(step, c // per)

    def plan_col_pass(step):
        wide = 8
        per = ntb // COL_PARTS // wide
        size = ns // ROW_PARTS
        for h in range(ROW_PARTS):
            receive_a(step, h)
            for c in range(ntb // wide):
                accs = [None] * wide
                for b in range(size // 64):
                    rows = slice(h * size + b * 64, h * size + (b + 1) * 64)
                    for k in range(wide):
                        lanes = slice((c * wide + k) * LANES, (c * wide + k + 1) * LANES)
                        ps = (plan[rows, lanes] * fcol[rows, :]).reshape(8, 8, LANES)
                        add = jnp.sum(ps, axis=0)
                        accs[k] = add if accs[k] is None else accs[k] + add
                for k in range(wide):
                    lanes = slice((c * wide + k) * LANES, (c * wide + k + 1) * LANES)
                    if h > 0:
                        accs[k] += col_p[:, lanes]
                    if h < ROW_PARTS - 1:
                        col_p[:, lanes] = accs[k]
                    else:
                        b_loc[step, c // per, c % per * wide + k : c % per * wide + k + 1, :] = jnp.sum(accs[k], axis=0, keepdims=True)
                if h == ROW_PARTS - 1 and c % per == per - 1:
                    send_cols(step, c // per)

    def send_cols(step, c):
        for peer in y_ids:
            copy(
                b_loc.at[step, c], b_y.at[step, c, y], s_by.at[step], r_by.at[step, c], peer
            ).start()

    def relay_cols(step, c):
        b_y[step, c, y] = b_loc[step, c]
        got = b_y.at[step, c, 0 : NY - 1]
        copy(got, got, s_by.at[step], r_by.at[step, c], peers[0]).wait_recv()
        parts = [b_y[step, c, i] for i in range(NY)]
        b_mid[step, c] = lse2(parts) if step == 0 else tree(jnp.add, parts)
        for peer in x_ids:
            copy(
                b_mid.at[step, c], b_x.at[step, c, x], s_bx.at[step], r_bx.at[step, c], peer
            ).start()

    def receive_b(step, c):
        b_x[step, c, x] = b_mid[step, c]
        got = b_x.at[step, c, 0 : NX - 1]
        copy(got, got, s_bx.at[step], r_bx.at[step, c], peers[0]).wait_recv()
        part = slice(c * (ntb // COL_PARTS), (c + 1) * (ntb // COL_PARTS))
        if step == 0:
            gpot[part, :] = -lse2([b_x[step, c, i] for i in range(NX)])
        else:
            fac = 1.0 / tree(jnp.add, [b_x[step, c, i] for i in range(NX)])
            g_out[part, :] = (
                gpot[part, :] + (jnp.log2(fac) + math.log2(n_src_total)) + ny[part, :]
            ) * UNSCALE
            for i in range(ntb // COL_PARTS):
                b = c * (ntb // COL_PARTS) + i
                rows = slice(b * LANES, (b + 1) * LANES)
                val = yt[rows, :] * jnp.broadcast_to(fac[i : i + 1, :], (LANES, LANES)).T
                v1 = val.astype(jnp.bfloat16)
                yv[rows, 0:LANES] = v1
                yv[rows, LANES : 2 * LANES] = (val - v1.astype(jnp.float32)).astype(jnp.bfloat16)

    order = sorted(range(NZ), key=lambda o: -hops(o, NZ))

    def split_plan():
        for t in range(NZ):
            base = pl.multiple_of((z + order[t]) % NZ * LANES, LANES)
            for q in range(LANES // 16):
                p = plan[pl.ds(pl.multiple_of(base + q * 16, 16), 16), :]
                p1 = p.astype(jnp.bfloat16)
                at = t * 2 * LANES + q * 16
                halves[at : at + 16, :] = p1
                halves[at + LANES : at + LANES + 16, :] = (
                    p - p1.astype(jnp.float32)
                ).astype(jnp.bfloat16)

    first_row_pass()
    build_map_operand()
    col_pass(0)
    for c in range(COL_PARTS):
        relay_cols(0, c)
    later_row_pass(1)
    plan_col_pass(1)
    split_plan()
    for c in range(COL_PARTS):
        relay_cols(1, c)

    half = d // 2
    partner = col_peer(0, 1)

    def product(t, count, c):
        part = slice(c * (nt // COL_PARTS), (c + 1) * (nt // COL_PARTS))
        rows = slice(t * 2 * LANES, (t + count) * 2 * LANES)
        both = jnp.dot(halves[rows, part], yv[part, :], preferred_element_type=jnp.float32)
        both = both[:, :LANES] + both[:, LANES:]
        out = []
        for i in range(count):
            at = i * 2 * LANES
            out.append(both[at : at + LANES] + both[at + LANES : at + 2 * LANES])
        return out

    for c in range(COL_PARTS - 1):
        receive_b(1, c)
        for t, res in enumerate(product(0, NZ, c)):
            m_acc[t] = res if c == 0 else m_acc[t] + res
    receive_b(1, COL_PARTS - 1)


    def finish_group(g):
        for i, res in enumerate(product(g * GROUP, GROUP, COL_PARTS - 1)):
            t = g * GROUP + i
            res = (res if COL_PARTS == 1 else m_acc[t] + res).T
            if order[t] == 0:
                c_in[z] = res[: d + 1]
            else:
                c_out[t] = res[: d + 1]
        for t in range(g * GROUP, (g + 1) * GROUP):
            if order[t] != 0:
                copy(c_out.at[t], c_in.at[z], s_c.at[0], r_c.at[0], col_peer(order[t], 0)).start()

    for g in range(NZ // GROUP):
        finish_group(g)
    got = c_in.at[0 : NZ - 1]
    c_whole = copy(got, got, s_c.at[0], r_c.at[0], peers[0])
    c_whole.wait_recv()
    tot = tree(jnp.add, [c_in[i] for i in range(NZ)])
    c_mine[0:half, :] = jnp.where(core == 0, tot[:half], tot[half:d])
    c_give[0:half, :] = jnp.where(core == 0, tot[half:d], tot[:half])
    c_mine[half : half + 1, :] = tot[d : d + 1]
    c_give[half : half + 1, :] = tot[d : d + 1]
    pair = copy(c_give, c_pair, s_p.at[0], r_p.at[0], partner)
    pair.start()
    pair.wait_recv()
    c_res[...] = (c_mine[0:half] + c_pair[0:half]) / (c_mine[half:] + c_pair[half:])

    def gather_copy(o, k):
        return copy(c_res, c_all.at[core, z], s_g.at[0], r_g.at[o, k], col_peer(o, k))

    def relay_copy(o):
        piece = c_all.at[core, (z + NZ - o) % NZ]
        return copy(piece, piece, s_g.at[0], r_g.at[o, 1], partner)

    direct = NZ // 2
    for o in order[:-1]:
        gather_copy(o, 0).start()
        if o == direct:
            gather_copy(o, 1).start()
    gather_copy(0, 1).start()
    c_all[core, z] = c_res[...]
    for o in order[::-1][1:-1]:
        gather_copy(o, 0).wait_recv()
        relay_copy(o).start()

    for step in range(ITERS):
        a_got = a_all.at[step, :, 0 : NC - 1]
        y_got, x_got = b_y.at[step, :, 0 : NY - 1], b_x.at[step, :, 0 : NX - 1]
        copy(a_got, a_got, s_a.at[step], r_a.at[step, 0], peers[0]).wait_send()
        copy(y_got, y_got, s_by.at[step], r_by.at[step, 0], peers[0]).wait_send()
        copy(x_got, x_got, s_bx.at[step], r_bx.at[step, 0], peers[0]).wait_send()
    pair.wait_send()
    c_whole.wait_send()
    gather_copy(direct, 0).wait_recv()
    for o in range(NZ):
        gather_copy(o, 1).wait_recv()
    for k in range(2):
        for i in range(NZ):
            m_out[k * half : (k + 1) * half, i * LANES : (i + 1) * LANES] = c_all[k, i]
    flat = c_all.at[0, 0 : NZ - 1]
    copy(c_all.at[0], c_all.at[0], s_g.at[0], r_g.at[0, 0], partner).wait_send()
    copy(flat, flat, s_g.at[0], r_g.at[0, 0], partner).wait_send()


def write_kernel(f, g, m, f_out, g_out, m_out, sems):
    copies = [
        pltpu.make_async_copy(a, b, sems.at[i])
        for i, (a, b) in enumerate(((m, m_out), (g, g_out), (f, f_out)))
    ]
    for c in copies:
        c.start()
    for c in copies:
        c.wait()


def solution(mesh):
    nrow, ncol = mesh.shape["row"], mesh.shape["col"]

    def shards(source, target):
        d, ns = source.shape
        nt = target.shape[1]
        nsb, ntb = ns // LANES, nt // LANES
        half = d // 2
        f32, bf16 = jnp.float32, jnp.bfloat16
        vmem = pltpu.VMEM
        dma = pltpu.SemaphoreType.DMA
        f, g, m = pl.pallas_call(
            functools.partial(kernel, ns * nrow, nt * ncol),
            out_shape=(
                jax.ShapeDtypeStruct((nsb, LANES), f32),
                jax.ShapeDtypeStruct((ntb, LANES), f32),
                jax.ShapeDtypeStruct((d, ns), f32),
            ),
            in_specs=[pl.BlockSpec(memory_space=pltpu.HBM)] * 2,
            out_specs=(pl.BlockSpec(memory_space=vmem),) * 3,
            scratch_shapes=[
                vmem((d, ns), f32),
                vmem((d, nt), f32),
                vmem((ns, 6 * d), bf16),
                vmem((6 * d, nt), bf16),
                vmem((nt, LANES), f32),
                vmem((nt, 2 * LANES), bf16),
                vmem((ns, nt), f32),
                vmem((ns, nt), f32),
                vmem((NZ * 2 * LANES, nt), bf16),
                vmem((NZ, LANES, LANES), f32),
                vmem((nsb, LANES), f32),
                vmem((ntb, LANES), f32),
                vmem((nsb, LANES), f32),
                vmem((ntb, LANES), f32),
                vmem((ns, LANES), f32),
                vmem((ns, LANES), f32),
                vmem((ns, LANES), f32),
                vmem((8, nt), f32),
                vmem((8, nt), f32),
                vmem((ITERS, ROW_PARTS, nsb // ROW_PARTS, LANES), f32),
                vmem((ITERS, ROW_PARTS, NC, nsb // ROW_PARTS, LANES), f32),
                vmem((ITERS, COL_PARTS, ntb // COL_PARTS, LANES), f32),
                vmem((ITERS, COL_PARTS, NY, ntb // COL_PARTS, LANES), f32),
                vmem((ITERS, COL_PARTS, ntb // COL_PARTS, LANES), f32),
                vmem((ITERS, COL_PARTS, NX, ntb // COL_PARTS, LANES), f32),
                vmem((half + 1, LANES), f32),
                vmem((half + 1, LANES), f32),
                vmem((half + 1, LANES), f32),
                vmem((NZ, d + 1, LANES), f32),
                vmem((NZ, d + 1, LANES), f32),
                vmem((half, LANES), f32),
                vmem((2, NZ, half, LANES), f32),
                dma((2,)),
                dma((ITERS,)),
                dma((ITERS, ROW_PARTS)),
                dma((ITERS,)),
                dma((ITERS, COL_PARTS)),
                dma((ITERS,)),
                dma((ITERS, COL_PARTS)),
                dma((1,)),
                dma((NZ,)),
                dma((1,)),
                dma((1,)),
                dma((1,)),
                dma((NZ, 2)),
            ],
            compiler_params=pltpu.CompilerParams(
                collective_id=0, has_side_effects=True, vmem_limit_bytes=VMEM_GRANT
            ),
            name="sinkhorn",
        )(source, target)
        f, g, m = pl.pallas_call(
            write_kernel,
            out_shape=(
                jax.ShapeDtypeStruct((nsb, LANES), f32),
                jax.ShapeDtypeStruct((ntb, LANES), f32),
                jax.ShapeDtypeStruct((d, ns), f32),
            ),
            in_specs=[pl.BlockSpec(memory_space=pl.ANY)] * 3,
            out_specs=(pl.BlockSpec(memory_space=pl.ANY),) * 3,
            scratch_shapes=[dma((3,))],
            compiler_params=pltpu.CompilerParams(vmem_limit_bytes=2**20),
            name="write_results",
        )(f, g, m)
        return f.reshape(ns), g.reshape(nt), m

    return jax.shard_map(
        shards,
        mesh=mesh,
        in_specs=(P(None, "row"), P(None, "col")),
        out_specs=(P("row"), P("col"), P(None, "row")),
        check_vma=False,
    )
```

```python
import functools
import math

import jax
import jax.numpy as jnp
from jax import lax
from jax.experimental import pallas as pl
from jax.experimental.pallas import tpu as pltpu
from jax.sharding import PartitionSpec as P

MESH = pl.DeviceIdType.MESH
ITERS = 2
EPSILON = 0.005
SCALE = 1.0 / (EPSILON * math.log(2.0))
UNSCALE = EPSILON * math.log(2.0)
LANES = 128
NZ, NX, NY = 8, 4, 8
NC = 2 * NZ
VMEM_GRANT = 56_150_000
ROW_PARTS, COL_PARTS = 2, 2
GROUP = 2


def normalize(points):
    total = jnp.sum(points * points, axis=0, keepdims=True)
    return points / jnp.sqrt(total + 1e-06)


def split3(a):
    a1 = a.astype(jnp.bfloat16)
    r = a - a1.astype(jnp.float32)
    a2 = r.astype(jnp.bfloat16)
    a3 = (r - a2.astype(jnp.float32)).astype(jnp.bfloat16)
    return a1, a2, a3


def tree(op, xs):
    xs = list(xs)
    while len(xs) > 1:
        xs = [op(xs[i], xs[i + 1]) if i + 1 < len(xs) else xs[i] for i in range(0, len(xs), 2)]
    return xs[0]


def lse2(xs):
    top = tree(jnp.maximum, xs)
    return top + jnp.log2(tree(jnp.add, [jnp.exp2(x - top) for x in xs]))


def hops(o, n):
    return min(o, n - o)


def kernel(
    n_src_total,
    n_tgt_total,
    src_hbm,
    tgt_hbm,
    f_out,
    g_out,
    m_out,
    src,
    tgt,
    xk,
    yk,
    yt,
    yv,
    score,
    plan,
    halves,
    m_acc,
    nx,
    ny,
    fpot,
    gpot,
    fcol,
    part_m,
    part_p,
    col_m,
    col_p,
    a_loc,
    a_all,
    b_loc,
    b_y,
    b_mid,
    b_x,
    c_mine,
    c_give,
    c_pair,
    c_sum,
    c_in,
    c_res,
    c_all,
    load,
    s_a,
    r_a,
    s_by,
    r_by,
    s_bx,
    r_bx,
    s_p,
    r_p,
    s_c,
    r_c,
    s_g,
    r_g,
):
    d, ns = src.shape
    nt = tgt.shape[1]
    nsb, ntb = ns // LANES, nt // LANES
    row, col = lax.axis_index("row"), lax.axis_index("col")
    y, x = row // NX, row % NX
    z, core = col // 2, col % 2

    load_src = pltpu.make_async_copy(src_hbm, src, load.at[0])
    load_tgt = pltpu.make_async_copy(tgt_hbm, tgt, load.at[1])
    load_src.start()
    load_tgt.start()

    col_peers = [(o, k) for o in range(NZ) for k in range(2) if (o, k) != (0, 0)]
    col_peers.sort(key=lambda p: -hops(p[0], NZ))
    y_peers = sorted(range(1, NY), key=lambda o: -hops(o, NY))
    x_peers = sorted(range(1, NX), key=lambda o: -hops(o, NX))

    def col_peer(o, k):
        return (row, ((z + o) % NZ) * 2 + (core + k) % 2)

    def y_peer(o):
        return (((y + o) % NY) * NX + x, col)

    def x_peer(o):
        return (y * NX + (x + o) % NX, col)

    col_ids = {p: col_peer(*p) for p in col_peers}
    y_ids = [y_peer(o) for o in y_peers]
    x_ids = [x_peer(o) for o in x_peers]
    peers = list(col_ids.values()) + y_ids + x_ids
    barrier = pltpu.get_barrier_semaphore()
    for peer in peers:
        pl.semaphore_signal(barrier, inc=1, device_id=peer, device_id_type=MESH)

    def copy(src_ref, dst_ref, send, recv, peer):
        return pltpu.make_async_remote_copy(
            src_ref=src_ref, dst_ref=dst_ref, send_sem=send, recv_sem=recv,
            device_id=peer, device_id_type=MESH,
        )

    load_src.wait()
    xs = normalize(src[...])
    nx_row = jnp.sum(xs * xs, axis=0, keepdims=True) * SCALE
    for b in range(nsb):
        nx[b : b + 1, :] = nx_row[:, b * LANES : (b + 1) * LANES]
    xs = xs * (2.0 * SCALE)
    first = lax.broadcasted_iota(jnp.int32, (LANES, LANES), 1) < d
    lane = lax.broadcasted_iota(jnp.int32, (LANES, LANES), 1)
    for b in range(nsb):
        blk = xs[:, b * LANES : (b + 1) * LANES]
        both = jnp.concatenate([blk, blk], axis=0).T
        x1 = both.astype(jnp.bfloat16).astype(jnp.float32)
        r = both - x1
        x2 = r.astype(jnp.bfloat16).astype(jnp.float32)
        rows = pl.ds(b * LANES, LANES)
        xk[rows, 0:128] = x1.astype(jnp.bfloat16)
        xk[rows, 128:256] = x2.astype(jnp.bfloat16)
        xk[rows, 256:384] = jnp.where(first, x1, r - x2).astype(jnp.bfloat16)
    load_tgt.wait()
    ys = normalize(tgt[...])
    tgt[...] = ys
    ny_row = jnp.sum(ys * ys, axis=0, keepdims=True) * SCALE
    for b in range(ntb):
        ny[b : b + 1, :] = ny_row[:, b * LANES : (b + 1) * LANES]
    y1, y2, y3 = split3(ys)
    for i, part in enumerate((y1, y2, y1, y2, y3, y1)):
        yk[i * d : (i + 1) * d, :] = part
    gpot[...] = -ny[...]

    def build_map_operand():
        for b in range(ntb):
            blk = tgt[:, b * LANES : (b + 1) * LANES]
            yt[b * LANES : (b + 1) * LANES, :] = jnp.concatenate(
                [blk, jnp.ones((LANES - d, LANES), jnp.float32)], axis=0
            ).T

    def score_tiles(c):
        rows = slice(c * 256, (c + 1) * 256)
        for n in range(nt // 256):
            lanes = slice(n * 256, (n + 1) * 256)

            def tile():
                score[rows, lanes] = jnp.dot(
                    xk[rows, :], yk[:, lanes], preferred_element_type=jnp.float32
                )

            yield tile

    def row_group(base, size):
        rows = pl.ds(base, size)
        ts = [score[rows, k * LANES : (k + 1) * LANES] + gpot[k : k + 1, :] for k in range(ntb)]
        top = tree(jnp.maximum, ts)
        part_m[rows, :] = top
        part_p[rows, :] = tree(jnp.add, [jnp.exp2(t - top) for t in ts])

    def add_source_potential():
        for b in range(ns // 32):
            rows = slice(b * 32, (b + 1) * 32)
            pot = fcol[rows, :]
            for k in range(ntb):
                lanes = slice(k * LANES, (k + 1) * LANES)
                score[rows, lanes] += pot

    def plan_group(base, size, lo, hi):
        rows = pl.ds(base, size)
        ps = []
        for k in range(lo, hi):
            lanes = slice(k * LANES, (k + 1) * LANES)
            p = jnp.exp2(score[rows, lanes] + gpot[k : k + 1, :])
            plan[rows, lanes] = p
            ps.append(p)
        tot = tree(jnp.add, ps)
        part_p[rows, :] = tot if lo == 0 else tot + part_p[rows, :]

    def send_rows(step, c):
        for i in range(nsb // ROW_PARTS):
            b = c * (nsb // ROW_PARTS) + i
            pt = part_p[b * LANES : (b + 1) * LANES, :].T
            if step == 0:
                mt = part_m[b * LANES : (b + 1) * LANES, :].T
                top = jnp.max(mt, axis=0, keepdims=True)
                tot = jnp.sum(pt * jnp.exp2(mt - top), axis=0, keepdims=True)
                a_loc[step, c, i : i + 1, :] = top + jnp.log2(tot)
            else:
                a_loc[step, c, i : i + 1, :] = jnp.sum(pt, axis=0, keepdims=True)
        if step == 0 and c == 0:
            pl.semaphore_wait(barrier, len(peers))
        for o, k in col_peers:
            copy(
                a_loc.at[step, c], a_all.at[step, c, col],
                s_a.at[step], r_a.at[step, c], col_peer(o, k),
            ).start()

    def first_row_pass():
        count = ns // 256
        for c in range(count + 1):
            tiles = score_tiles(c) if c < count else [lambda: None] * (nt // 256)
            for n, tile in enumerate(tiles):
                tile()
                if c > 0:
                    for q in range(2):
                        row_group((c - 1) * 256 + n * 32 + q * 16, 16)
            if c > 0 and c % (count // ROW_PARTS) == 0:
                send_rows(0, c // (count // ROW_PARTS) - 1)

    def later_row_pass(step):
        wide = ntb // COL_PARTS
        tall = 256 // wide
        for c in range(COL_PARTS):
            receive_b(step - 1, c)
            size = ns // ROW_PARTS
            for h in range(ROW_PARTS):

                def group(q, _):
                    base = pl.multiple_of(h * size + q * tall, tall)
                    plan_group(base, tall, c * wide, (c + 1) * wide)
                    return 0

                lax.fori_loop(0, size // tall, group, 0, unroll=8)
                if c == COL_PARTS - 1:
                    send_rows(step, h)

    def receive_a(step, c):
        a_all[step, c, col] = a_loc[step, c]
        got = a_all.at[step, c, 0 : NC - 1]
        copy(got, got, s_a.at[step], r_a.at[step, c], peers[0]).wait_recv()
        size = nsb // ROW_PARTS
        part = slice(c * size, (c + 1) * size)
        if step == 0:
            pot = math.log2(n_tgt_total) - lse2([a_all[step, c, i] for i in range(NC)])
            fpot[part, :] = pot
        else:
            tot = tree(jnp.add, [a_all[step, c, i] for i in range(NC)])
            pot = (n_tgt_total / n_src_total) / tot
            f_out[part, :] = (fpot[part, :] + jnp.log2(pot) + nx[part, :]) * UNSCALE
        for i in range(size):
            b = c * size + i
            fcol[b * LANES : (b + 1) * LANES, :] = jnp.broadcast_to(
                pot[i : i + 1, :], (LANES, LANES)
            ).T

    def col_pass(step):
        wide = 8
        per = ntb // COL_PARTS // wide
        size = ns // ROW_PARTS
        for h in range(ROW_PARTS):
            receive_a(step, h)
            for c in range(ntb // wide):
                tops, accs = [None] * wide, [None] * wide
                if h > 0:
                    for k in range(wide):
                        lanes = slice((c * wide + k) * LANES, (c * wide + k + 1) * LANES)
                        tops[k], accs[k] = col_m[:, lanes], col_p[:, lanes]
                for b in range(size // 64):
                    for k in range(wide):
                        lanes = slice((c * wide + k) * LANES, (c * wide + k + 1) * LANES)
                        rows = slice(h * size + b * 64, h * size + (b + 1) * 64)
                        ts = (score[rows, lanes] + fcol[rows, :]).reshape(8, 8, LANES)
                        new = jnp.max(ts, axis=0)
                        if tops[k] is not None:
                            new = jnp.maximum(new, tops[k])
                        add = jnp.sum(jnp.exp2(ts - new[None]), axis=0)
                        if tops[k] is not None:
                            add += accs[k] * jnp.exp2(tops[k] - new)
                        tops[k], accs[k] = new, add
                for k in range(wide):
                    if h < ROW_PARTS - 1:
                        lanes = slice((c * wide + k) * LANES, (c * wide + k + 1) * LANES)
                        col_m[:, lanes], col_p[:, lanes] = tops[k], accs[k]
                    else:
                        full = jnp.max(tops[k], axis=0, keepdims=True)
                        tot = jnp.sum(accs[k] * jnp.exp2(tops[k] - full), axis=0, keepdims=True)
                        b_loc[step, c // per, c % per * wide + k : c % per * wide + k + 1, :] = full + jnp.log2(tot)
                if h == ROW_PARTS - 1 and c % per == per - 1:
                    send_cols(step, c // per)

    def plan_col_pass(step):
        wide = 8
        per = ntb // COL_PARTS // wide
        size = ns // ROW_PARTS
        for h in range(ROW_PARTS):
            receive_a(step, h)
            for c in range(ntb // wide):
                accs = [None] * wide
                for b in range(size // 64):
                    rows = slice(h * size + b * 64, h * size + (b + 1) * 64)
                    for k in range(wide):
                        lanes = slice((c * wide + k) * LANES, (c * wide + k + 1) * LANES)
                        ps = (plan[rows, lanes] * fcol[rows, :]).reshape(8, 8, LANES)
                        add = jnp.sum(ps, axis=0)
                        accs[k] = add if accs[k] is None else accs[k] + add
                for k in range(wide):
                    lanes = slice((c * wide + k) * LANES, (c * wide + k + 1) * LANES)
                    if h > 0:
                        accs[k] += col_p[:, lanes]
                    if h < ROW_PARTS - 1:
                        col_p[:, lanes] = accs[k]
                    else:
                        b_loc[step, c // per, c % per * wide + k : c % per * wide + k + 1, :] = jnp.sum(accs[k], axis=0, keepdims=True)
                if h == ROW_PARTS - 1 and c % per == per - 1:
                    send_cols(step, c // per)

    def send_cols(step, c):
        for peer in y_ids:
            copy(
                b_loc.at[step, c], b_y.at[step, c, y], s_by.at[step], r_by.at[step, c], peer
            ).start()

    def relay_cols(step, c):
        b_y[step, c, y] = b_loc[step, c]
        got = b_y.at[step, c, 0 : NY - 1]
        copy(got, got, s_by.at[step], r_by.at[step, c], peers[0]).wait_recv()
        parts = [b_y[step, c, i] for i in range(NY)]
        b_mid[step, c] = lse2(parts) if step == 0 else tree(jnp.add, parts)
        for peer in x_ids:
            copy(
                b_mid.at[step, c], b_x.at[step, c, x], s_bx.at[step], r_bx.at[step, c], peer
            ).start()

    def receive_b(step, c):
        b_x[step, c, x] = b_mid[step, c]
        got = b_x.at[step, c, 0 : NX - 1]
        copy(got, got, s_bx.at[step], r_bx.at[step, c], peers[0]).wait_recv()
        part = slice(c * (ntb // COL_PARTS), (c + 1) * (ntb // COL_PARTS))
        if step == 0:
            gpot[part, :] = -lse2([b_x[step, c, i] for i in range(NX)])
        else:
            fac = 1.0 / tree(jnp.add, [b_x[step, c, i] for i in range(NX)])
            g_out[part, :] = (
                gpot[part, :] + (jnp.log2(fac) + math.log2(n_src_total)) + ny[part, :]
            ) * UNSCALE
            for i in range(ntb // COL_PARTS):
                b = c * (ntb // COL_PARTS) + i
                rows = slice(b * LANES, (b + 1) * LANES)
                val = yt[rows, :] * jnp.broadcast_to(fac[i : i + 1, :], (LANES, LANES)).T
                v1 = val.astype(jnp.bfloat16)
                yv[rows, 0:LANES] = v1
                yv[rows, LANES : 2 * LANES] = (val - v1.astype(jnp.float32)).astype(jnp.bfloat16)

    order = sorted(range(NZ), key=lambda o: -hops(o, NZ))

    def split_plan():
        for t in range(NZ):
            base = pl.multiple_of((z + order[t]) % NZ * LANES, LANES)
            for q in range(LANES // 16):
                p = plan[pl.ds(pl.multiple_of(base + q * 16, 16), 16), :]
                p1 = p.astype(jnp.bfloat16)
                at = t * 2 * LANES + q * 16
                halves[at : at + 16, :] = p1
                halves[at + LANES : at + LANES + 16, :] = (
                    p - p1.astype(jnp.float32)
                ).astype(jnp.bfloat16)

    first_row_pass()
    build_map_operand()
    col_pass(0)
    add_source_potential()
    for c in range(COL_PARTS):
        relay_cols(0, c)
    later_row_pass(1)
    plan_col_pass(1)
    split_plan()
    for c in range(COL_PARTS):
        relay_cols(1, c)

    half = d // 2
    partner = col_peer(0, 1)

    def product(t, count, c):
        part = slice(c * (nt // COL_PARTS), (c + 1) * (nt // COL_PARTS))
        rows = slice(t * 2 * LANES, (t + count) * 2 * LANES)
        both = jnp.dot(halves[rows, part], yv[part, :], preferred_element_type=jnp.float32)
        both = both[:, :LANES] + both[:, LANES:]
        out = []
        for i in range(count):
            at = i * 2 * LANES
            out.append(both[at : at + LANES] + both[at + LANES : at + 2 * LANES])
        return out

    for c in range(COL_PARTS - 1):
        receive_b(1, c)
        for t, res in enumerate(product(0, NZ, c)):
            m_acc[t] = res if c == 0 else m_acc[t] + res
    receive_b(1, COL_PARTS - 1)


    def pair_copy(g):
        part = pl.ds(g * GROUP, GROUP)
        return copy(c_give.at[part], c_pair.at[part], s_p.at[0], r_p.at[g], partner)

    def finish_group(g):
        for i, res in enumerate(product(g * GROUP, GROUP, COL_PARTS - 1)):
            t = g * GROUP + i
            res = (res if COL_PARTS == 1 else m_acc[t] + res).T
            c_mine[t, 0:half, :] = jnp.where(core == 0, res[:half], res[half:d])
            c_give[t, 0:half, :] = jnp.where(core == 0, res[half:d], res[:half])
            c_mine[t, half : half + 1, :] = res[d : d + 1]
            c_give[t, half : half + 1, :] = res[d : d + 1]
        pair_copy(g).start()

    def merge_group(g):
        pair_copy(g).wait_recv()
        for t in range(g * GROUP, (g + 1) * GROUP):
            if order[t] == 0:
                c_in[z] = c_mine[t] + c_pair[t]
            else:
                c_sum[t] = c_mine[t] + c_pair[t]
        for t in range(g * GROUP, (g + 1) * GROUP):
            if order[t] != 0:
                copy(c_sum.at[t], c_in.at[z], s_c.at[0], r_c.at[0], col_peer(order[t], 0)).start()

    for g in range(NZ // GROUP):
        finish_group(g)
        if g > 0:
            merge_group(g - 1)
    merge_group(NZ // GROUP - 1)
    got = c_in.at[0 : NZ - 1]
    c_whole = copy(got, got, s_c.at[0], r_c.at[0], peers[0])
    c_whole.wait_recv()
    tot = tree(jnp.add, [c_in[i] for i in range(NZ)])
    c_res[...] = tot[:half] / tot[half : half + 1]

    def gather_copy(o, k):
        return copy(c_res, c_all.at[core, z], s_g.at[0], r_g.at[o, k], col_peer(o, k))

    def relay_copy(o):
        piece = c_all.at[core, (z + NZ - o) % NZ]
        return copy(piece, piece, s_g.at[0], r_g.at[o, 1], partner)

    direct = [o for o in order if hops(o, NZ) > 2]
    for o in order[:-1]:
        gather_copy(o, 0).start()
        if o in direct:
            gather_copy(o, 1).start()
    gather_copy(0, 1).start()
    c_all[core, z] = c_res[...]
    for o in [o for o in order[::-1] if o != 0 and o not in direct]:
        gather_copy(o, 0).wait_recv()
        relay_copy(o).start()

    for step in range(ITERS):
        a_got = a_all.at[step, :, 0 : NC - 1]
        y_got, x_got = b_y.at[step, :, 0 : NY - 1], b_x.at[step, :, 0 : NX - 1]
        copy(a_got, a_got, s_a.at[step], r_a.at[step, 0], peers[0]).wait_send()
        copy(y_got, y_got, s_by.at[step], r_by.at[step, 0], peers[0]).wait_send()
        copy(x_got, x_got, s_bx.at[step], r_bx.at[step, 0], peers[0]).wait_send()
    copy(c_give, c_give, s_p.at[0], r_p.at[0], partner).wait_send()
    c_whole.wait_send()
    for o in direct:
        gather_copy(o, 0).wait_recv()
    for o in range(NZ):
        gather_copy(o, 1).wait_recv()
    for k in range(2):
        for i in range(NZ):
            m_out[k * half : (k + 1) * half, i * LANES : (i + 1) * LANES] = c_all[k, i]
    flat = c_all.at[0, 0 : NZ - 1]
    copy(c_all.at[0], c_all.at[0], s_g.at[0], r_g.at[0, 0], partner).wait_send()
    copy(flat, flat, s_g.at[0], r_g.at[0, 0], partner).wait_send()


def write_kernel(f, g, m, f_out, g_out, m_out, sems):
    copies = [
        pltpu.make_async_copy(a, b, sems.at[i])
        for i, (a, b) in enumerate(((m, m_out), (g, g_out), (f, f_out)))
    ]
    for c in copies:
        c.start()
    for c in copies:
        c.wait()


def solution(mesh):
    nrow, ncol = mesh.shape["row"], mesh.shape["col"]

    def shards(source, target):
        d, ns = source.shape
        nt = target.shape[1]
        nsb, ntb = ns // LANES, nt // LANES
        half = d // 2
        f32, bf16 = jnp.float32, jnp.bfloat16
        vmem = pltpu.VMEM
        dma = pltpu.SemaphoreType.DMA
        f, g, m = pl.pallas_call(
            functools.partial(kernel, ns * nrow, nt * ncol),
            out_shape=(
                jax.ShapeDtypeStruct((nsb, LANES), f32),
                jax.ShapeDtypeStruct((ntb, LANES), f32),
                jax.ShapeDtypeStruct((d, ns), f32),
            ),
            in_specs=[pl.BlockSpec(memory_space=pltpu.HBM)] * 2,
            out_specs=(pl.BlockSpec(memory_space=vmem),) * 3,
            scratch_shapes=[
                vmem((d, ns), f32),
                vmem((d, nt), f32),
                vmem((ns, 6 * d), bf16),
                vmem((6 * d, nt), bf16),
                vmem((nt, LANES), f32),
                vmem((nt, 2 * LANES), bf16),
                vmem((ns, nt), f32),
                vmem((ns, nt), f32),
                vmem((NZ * 2 * LANES, nt), bf16),
                vmem((NZ, LANES, LANES), f32),
                vmem((nsb, LANES), f32),
                vmem((ntb, LANES), f32),
                vmem((nsb, LANES), f32),
                vmem((ntb, LANES), f32),
                vmem((ns, LANES), f32),
                vmem((ns, LANES), f32),
                vmem((ns, LANES), f32),
                vmem((8, nt), f32),
                vmem((8, nt), f32),
                vmem((ITERS, ROW_PARTS, nsb // ROW_PARTS, LANES), f32),
                vmem((ITERS, ROW_PARTS, NC, nsb // ROW_PARTS, LANES), f32),
                vmem((ITERS, COL_PARTS, ntb // COL_PARTS, LANES), f32),
                vmem((ITERS, COL_PARTS, NY, ntb // COL_PARTS, LANES), f32),
                vmem((ITERS, COL_PARTS, ntb // COL_PARTS, LANES), f32),
                vmem((ITERS, COL_PARTS, NX, ntb // COL_PARTS, LANES), f32),
                vmem((NZ, half + 1, LANES), f32),
                vmem((NZ, half + 1, LANES), f32),
                vmem((NZ, half + 1, LANES), f32),
                vmem((NZ, half + 1, LANES), f32),
                vmem((NZ, half + 1, LANES), f32),
                vmem((half, LANES), f32),
                vmem((2, NZ, half, LANES), f32),
                dma((2,)),
                dma((ITERS,)),
                dma((ITERS, ROW_PARTS)),
                dma((ITERS,)),
                dma((ITERS, COL_PARTS)),
                dma((ITERS,)),
                dma((ITERS, COL_PARTS)),
                dma((1,)),
                dma((NZ,)),
                dma((1,)),
                dma((1,)),
                dma((1,)),
                dma((NZ, 2)),
            ],
            compiler_params=pltpu.CompilerParams(
                collective_id=0, has_side_effects=True, vmem_limit_bytes=VMEM_GRANT
            ),
            name="sinkhorn",
        )(source, target)
        f, g, m = pl.pallas_call(
            write_kernel,
            out_shape=(
                jax.ShapeDtypeStruct((nsb, LANES), f32),
                jax.ShapeDtypeStruct((ntb, LANES), f32),
                jax.ShapeDtypeStruct((d, ns), f32),
            ),
            in_specs=[pl.BlockSpec(memory_space=pl.ANY)] * 3,
            out_specs=(pl.BlockSpec(memory_space=pl.ANY),) * 3,
            scratch_shapes=[dma((3,))],
            compiler_params=pltpu.CompilerParams(vmem_limit_bytes=2**20),
            name="write_results",
        )(f, g, m)
        return f.reshape(ns), g.reshape(nt), m

    return jax.shard_map(
        shards,
        mesh=mesh,
        in_specs=(P(None, "row"), P(None, "col")),
        out_specs=(P("row"), P("col"), P(None, "row")),
        check_vma=False,
    )
```
